32 devices in a mesh: group: 2 (over x), patch: 16 (over z, y, core).
Axes of the slice: x: 2, y: 2, z: 4, core: 2. Of those that a mesh axis runs over, the one named last changes fastest.
Arguments:
- features: bfloat16 [32, 64, 4, 2304], P(('group', 'patch')), parts along dimension 0, may hold values from -6 to 6
- w_in: bfloat16 [28, 64], replicated, may hold values from -0.75 to 0.75
- w_plane: bfloat16 [9, 28, 28], replicated, may hold values from -0.375 to 0.375
- w_depth: bfloat16 [3, 28, 28], replicated, may hold values from -0.625 to 0.625
- w_head: bfloat16 [3, 28], replicated, may hold values from -1 to 1
- brick_owner: int32 [32], P(('group', 'patch')), parts along dimension 0, may hold values from 0 to 15, each once
- patch_anchor: int32 [32], P(('group', 'patch')), parts along dimension 0, may hold values from 0 to 3, as said below
- aug_code: int32 [32], P(('group', 'patch')), parts along dimension 0, may hold values from 0 to 7, as said below
Outputs:
- blended: float32 [32, 4, 2304], P(('group', 'patch')), parts along dimension 0
The draws below stay inside these ranges and needn't reach their ends.
There are 2 independent parts, one for each index of `group`. The reference program is written for one: setup_inputs(seed, part) draws one part's arguments, and reference() takes and returns one part's arrays. A program takes and returns all parts, laid end to end along the dimension named above; an argument that names none is the same for every part. Nothing has to cross between parts.
Inputs may be any that keep to these rules, and one draw needn't show every extreme that they name: `brick_owner`: every device owns exactly one brick of its region. `patch_anchor`: devices 8 k to 8 k + 7 share one anchor; different positions have different anchors. `aug_code`: devices 8 k to 8 k + 7 hold each code once.
All inputs are finite; a program needn't handle non-finite values.
Results may differ from the reference program's by a relative error of at most 0.00048.
Values sent between devices are 32-bit elements; how exact they have to be, the bound alone decides.
A program may use at most 64 MiB of HBM per device.

```python
import math
import jax
import jax.numpy as jnp
from jax import lax

CIN = 64
CH = 28
PZ = 4
AUGS = 8
HALF = 48
POSITIONS = 2
NB_Y = 4
N_PATCH = 16


def draw_patch_anchor(key, part):
    row_order = jax.random.permutation(key, NB_Y)
    anchor_rows = row_order[:POSITIONS]
    return jnp.repeat(anchor_rows, AUGS).astype(jnp.int32)


def draw_aug_code(key, part):
    split_keys = jax.random.split(jax.random.fold_in(key, 7), POSITIONS)
    orderings = jax.vmap(lambda one_key: jax.random.permutation(one_key, AUGS))(split_keys)
    return orderings.reshape(-1).astype(jnp.int32)


def block_scale(own_key, extent, shards, low, top_value):
    def one(axis_at, parts):
        heights = jax.random.uniform(jax.random.fold_in(jax.random.fold_in(own_key, 6), axis_at), (parts,), jnp.float32, low / len(shards), top_value / len(shards))
        return jnp.repeat(jnp.exp(heights), extent[axis_at] // parts).reshape((-1,) + (1,) * (len(extent) - axis_at - 1))

    level = one(*shards[0])
    for cut in shards[1:]:
        level = level * one(*cut)
    return level


def scatter_about(rng, shape, width, bound, cuts=(), held_as=jnp.bfloat16):
    values = width * jax.random.normal(rng, shape, jnp.float32)
    if cuts:
        values = values * block_scale(rng, shape, cuts, -0.22, 0.18)
    return jnp.clip(values, -bound, bound).astype(held_as)


def setup_inputs(seed: int = 0, part: int = 0) -> dict:
    seeds = jax.random.split(jax.random.key(seed), 9)
    own_keys = jax.random.split(jax.random.fold_in(seeds[8], part), 9)
    features = scatter_about(own_keys[0], (N_PATCH, CIN, PZ, HALF * HALF), 1.0, 6.0, ((0, 16),))
    w_in = scatter_about(seeds[1], (CH, CIN), CIN ** -0.5, 0.75)
    w_plane = scatter_about(seeds[2], (9, CH, CH), (9 * CH) ** -0.5, 0.375)
    w_depth = scatter_about(seeds[3], (3, CH, CH), (3 * CH) ** -0.5, 0.625)
    w_head = scatter_about(seeds[4], (3, CH), CH ** -0.5, 1.0)
    brick_owner = jax.random.permutation(own_keys[5], N_PATCH).astype(jnp.int32)
    patch_anchor = draw_patch_anchor(jax.random.fold_in(jax.random.fold_in(seeds[8], part), 71), part)
    aug_code = draw_aug_code(jax.random.fold_in(jax.random.fold_in(seeds[8], part), 71), part)
    return {"features": features, "w_in": w_in, "w_plane": w_plane, "w_depth": w_depth, "w_head": w_head, "brick_owner": brick_owner, "patch_anchor": patch_anchor, "aug_code": aug_code}


def bump_curve(length):
    position = (jnp.arange(length, dtype=jnp.float32) + 0.5) / length
    return 0.1 + jnp.sin(jnp.pi * position) ** 2

def window_volume(patch_depth, plane_side):
    return bump_curve(patch_depth)[:, None, None] * bump_curve(plane_side)[None, :, None] * bump_curve(plane_side)[None, None, :]

def brick_partition(volume, brick_side):
    channels, patch_depth = (volume.shape[0], volume.shape[1])
    blocks = volume.reshape(channels, patch_depth, 4, brick_side, 4, brick_side).transpose(2, 4, 0, 1, 3, 5)
    return blocks.reshape(16, channels, patch_depth * brick_side * brick_side)

def mix_channels(weights, values):
    return jnp.einsum('oi,izyx->ozyx', weights.astype(jnp.float32), values.astype(jnp.float32), precision=lax.Precision.HIGHEST)

def patch_output(patch_feat, flip_code, w_in, w_plane, w_depth, w_head):
    channels, patch_depth, half_plane = patch_feat.shape
    half_side = math.isqrt(half_plane)
    plane_side = 2 * half_side
    brick_side = plane_side // 4
    hidden = w_in.shape[0]
    coarse = patch_feat.reshape(channels, patch_depth, half_side, half_side)
    projected = mix_channels(w_in, coarse).astype(jnp.bfloat16)
    upsampled = jnp.repeat(jnp.repeat(projected, 2, axis=2), 2, axis=3)
    padded = jnp.pad(upsampled, ((0, 0), (0, 0), (1, 1), (1, 1)))
    mix_total = jnp.zeros((hidden, patch_depth, plane_side, plane_side), jnp.float32)
    for row_tap in range(3):
        for col_tap in range(3):
            window_in = padded[:, :, row_tap:row_tap + plane_side, col_tap:col_tap + plane_side]
            mix_total = mix_total + mix_channels(w_plane[3 * row_tap + col_tap], window_in)
    first_out = (upsampled.astype(jnp.float32) + jax.nn.relu(mix_total)).astype(jnp.bfloat16)
    padded_depth = jnp.pad(first_out, ((0, 0), (1, 1), (0, 0), (0, 0)))
    mix_total = jnp.zeros((hidden, patch_depth, plane_side, plane_side), jnp.float32)
    for depth_tap in range(3):
        mix_total = mix_total + mix_channels(w_depth[depth_tap], padded_depth[:, depth_tap:depth_tap + patch_depth])
    second_out = (first_out.astype(jnp.float32) + jax.nn.relu(mix_total)).astype(jnp.bfloat16)
    affinity = jax.nn.sigmoid(mix_channels(w_head, second_out))
    affinity = jnp.where(flip_code % 2 == 1, affinity[:, ::-1], affinity)
    affinity = jnp.where(flip_code // 2 % 2 == 1, affinity[:, :, ::-1], affinity)
    affinity = jnp.where(flip_code // 4 % 2 == 1, affinity[:, :, :, ::-1], affinity)
    window = window_volume(patch_depth, plane_side)
    weighted = jnp.concatenate([affinity * window[None], window[None]], axis=0)
    return brick_partition(weighted, brick_side)

def reference(features, w_in, w_plane, w_depth, w_head, brick_owner, patch_anchor, aug_code):
    devices = features.shape[0]
    brick_rows = devices // 4
    cells = features.shape[2] * features.shape[3] // 4
    tile_index = jnp.arange(16, dtype=jnp.int32)

    def add_patch(running, patch_item):
        patch_feat, anchor_row, flip_code = patch_item
        volume_bricks = patch_output(patch_feat, flip_code, w_in, w_plane, w_depth, w_head)
        brick_id = ((anchor_row + tile_index // 4) % brick_rows * 4 + tile_index % 4).astype(jnp.int32)
        owners = brick_owner[brick_id]
        return (running.at[owners].add(volume_bricks), None)
    start = jnp.zeros((devices, 4, cells), jnp.float32)
    blended, _ = lax.scan(add_patch, start, (features, patch_anchor, aug_code))
    return blended
```

```python
import functools
import math

import jax
import jax.numpy as jnp
import numpy as np
from jax import lax
from jax.experimental import pallas as pl
from jax.experimental.pallas import tpu as pltpu
from jax.sharding import PartitionSpec as P

MESH = pl.DeviceIdType.MESH
LANES = 128
PAD = 32
F32 = jnp.float32
BF16 = jnp.bfloat16


def bump(length):
    position = (np.arange(length) + 0.5) / length
    return 0.1 + np.sin(np.pi * position) ** 2


def tables(half, depth):
    hb = half // 4
    cells = hb * hb
    rest = cells - LANES
    block = hb * half
    side = 2 * half
    fine = 4 * cells
    yc, xc = np.divmod(np.arange(cells), hb)
    groups = LANES // rest
    place = np.zeros((4, block, 8 * LANES), np.float32)
    for flip in range(4):
        fy, fx = flip % 2, flip // 2
        for j in range(4):
            ys = hb - 1 - yc if fy else yc
            xs = half - 1 - (hb * j + xc) if fx else hb * j + xc
            lane = ys * half + xs
            m = np.arange(LANES)
            place[flip, lane[:LANES], j * LANES + m] = 1
            for g in range(groups):
                place[flip, lane[LANES:], (4 + j) * LANES + rest * g + np.arange(rest)] = 1
    spread = np.zeros((2, 4 * LANES, fine), np.float32)
    for py in range(2):
        for px in range(2):
            cell = (2 * yc + py) * (2 * hb) + 2 * xc + px
            spread[py, px * LANES + np.arange(LANES), cell[:LANES]] = 1
            for g in range(groups):
                spread[py, (2 + px) * LANES + rest * g + np.arange(rest), cell[LANES:]] = 1
    bz, by = bump(depth), bump(side)
    win = np.zeros((16, 24, LANES), np.float32)
    win_out = np.zeros((16, 1, depth * fine), np.float32)
    for i in range(4):
        for j in range(4):
            rows = by[2 * hb * i : 2 * hb * (i + 1)]
            cols = by[2 * hb * j : 2 * hb * (j + 1)]
            win_out[i * 4 + j, 0] = (bz[:, None, None] * rows[None, :, None] * cols[None, None, :]).reshape(-1)
            for py in range(2):
                for px in range(2):
                    value = bz[:, None] * (rows[2 * yc + py] * cols[2 * xc + px])[None]
                    win[i * 4 + j, 8 * py + px * 4 : 8 * py + px * 4 + 4] = value[:, :LANES]
                    for k in range(3):
                        at = rest * (3 * py + k)
                        win[i * 4 + j, 16 + px * 4 : 20 + px * 4, at : at + rest] = value[:, LANES:]
    return (
        jnp.asarray(place, BF16),
        jnp.asarray(spread, BF16),
        jnp.asarray(win, F32),
        jnp.asarray(win_out, F32),
    )


def shifted(values, offset):
    rows, length = values.shape
    zeros = jnp.zeros((rows, abs(offset)), values.dtype)
    if offset > 0:
        return jnp.concatenate([values[:, offset:], zeros], axis=1)
    return jnp.concatenate([zeros, values[:, : length + offset]], axis=1)


def dot(a, b):
    return jnp.dot(a, b, preferred_element_type=F32)


def split(values):
    high = values.astype(BF16)
    return high, (values - high.astype(F32)).astype(BF16)


def kernel(
    n, half,
    feat, w_in, w_plane, w_depth, w_head, owner_s, anchor_s, code_s, place_h, spread_h, win_h, win_out_h,
    out,
    place, spread, win, win_out, table_sem,
    wi_s, wp_s, wd_s, wh_s, xs, first_s, second_s, br0, br1,
    say, heard, inverse_v, inverse_s, inverse_sem, say_sem, hear_sem,
    pair_out0, pair_in0, kept0, cross_out0, cross_in0,
    pair_out1, pair_in1, kept1, cross_out1, cross_in1,
    pair_send, pair_recv, cross_send, cross_recv,
):
    hidden = w_in.shape[0]
    cin = w_in.shape[1]
    depth = feat.shape[2]
    plane = half * half
    block = plane // 4
    chips = n // 2
    brick_rows = n // 4
    rest = plane // 16 - LANES
    fine = plane // 4
    me = lax.axis_index("patch")
    chip, core = me // 2, lax.rem(me, 2)
    partner = me + 1 - 2 * core

    loads = [
        pltpu.make_async_copy(h, v, table_sem.at[s])
        for s, (h, v) in enumerate(((place_h, place), (win_h, win), (spread_h, spread), (win_out_h, win_out)))
    ]
    for load in loads:
        load.start()

    barrier = pltpu.get_barrier_semaphore()
    for off in range(1, n):
        pl.semaphore_signal(barrier, inc=1, device_id={"patch": lax.rem(me + off, n)}, device_id_type=MESH)

    code = code_s[0]
    anchor = anchor_s[0]
    fz, fy, fx = code % 2, (code // 2) % 2, code // 4
    word = jnp.concatenate(
        [jnp.full((1, LANES), owner_s[0], jnp.int32), jnp.full((1, LANES), anchor, jnp.int32)], axis=0
    )
    say[...] = word
    heard[me] = word

    spread_cols = lax.broadcasted_iota(jnp.int32, (cin, cin * depth), 1) // depth
    spread_rows = lax.broadcasted_iota(jnp.int32, (cin, cin * depth), 0)
    wi_all = dot(w_in[...], (spread_cols == spread_rows).astype(F32).astype(BF16))
    section = lax.broadcasted_iota(jnp.int32, (hidden, cin * depth), 1) % depth
    wi_s[...] = jnp.zeros_like(wi_s)
    for z in range(depth):
        wi_s[PAD * z : PAD * z + hidden, :] = jnp.where(section == z, wi_all, 0.0)
    wp_s[...] = jnp.zeros_like(wp_s)
    taps = [w_plane[t].astype(F32) for t in range(9)]
    halves = (((0,), (1, 2)), ((0, 1), (2,)))
    for sy in range(2):
        for dyi in range(2):
            for px in range(2):
                for at, txs in enumerate(halves[px]):
                    total = sum(taps[3 * ty + tx] for ty in halves[sy][dyi] for tx in txs)
                    col = PAD * (3 * dyi + px + at)
                    wp_s[sy, PAD * px : PAD * px + hidden, col : col + hidden] = total
    wd_s[...] = jnp.zeros_like(wd_s)
    for z in range(depth):
        for tz in range(3):
            if 0 <= z + tz - 1 < depth:
                col = PAD * (z + tz - 1)
                wd_s[PAD * z : PAD * z + hidden, col : col + hidden] = w_depth[tz].astype(F32)
    wh_s[...] = jnp.zeros_like(wh_s)
    for m in range(2 * depth):
        wh_s[:, PAD * m : PAD * m + hidden] = w_head[...].astype(F32)
    row8 = lax.broadcasted_iota(jnp.int32, (8, 2 * depth * PAD), 0)
    col8 = lax.broadcasted_iota(jnp.int32, (8, 2 * depth * PAD), 1) // PAD
    z_from = jnp.where(fz == 1, depth - 1 - col8 % depth, col8 % depth)
    px_from = jnp.where(fx == 1, 1 - col8 // depth, col8 // depth)
    wanted = row8 == px_from * depth + z_from
    head = jnp.concatenate(
        [jnp.where(wanted, jnp.broadcast_to(wh_s[k : k + 1, :], wanted.shape), 0.0) for k in range(3)], axis=0
    ).astype(BF16)
    depth_w = wd_s[...].astype(BF16)

    x = dot(wi_s[...].astype(BF16), feat[0].reshape(cin * depth, plane)).astype(BF16)
    lane_x = lax.broadcasted_iota(jnp.int32, (1, plane), 1) % half
    left = shifted(x, -1) * (lane_x >= 1).astype(F32).astype(BF16)
    right = shifted(x, 1) * (lane_x <= half - 2).astype(F32).astype(BF16)
    for dx, values in enumerate((left, x, right)):
        xs[0, dx] = shifted(values, -half)
        xs[1, dx] = values
        xs[2, dx] = shifted(values, half)

    pl.semaphore_wait(barrier, n - 1)
    tells = []
    for off in range(1, n):
        tells.append(
            pltpu.make_async_remote_copy(
                src_ref=say, dst_ref=heard.at[me], send_sem=say_sem.at[off - 1], recv_sem=hear_sem.at[off - 1],
                device_id={"patch": lax.rem(me + off, n)}, device_id_type=MESH,
            )
        )
        tells[-1].start()

    lane = lax.broadcasted_iota(jnp.int32, (8, LANES), 1) // rest

    def planes(qy):
        sy = jnp.where(fy == 1, 1 - qy, qy)
        w_high, w_low = split(wp_s[sy])
        weights = jnp.concatenate([w_high, w_low], axis=0)
        around = [xs[sy + dyi, dx] for dyi in range(2) for dx in range(3)]
        for z in range(depth):
            rows = slice(PAD * z, PAD * (z + 1))
            mixed = dot(weights, jnp.concatenate([a[rows] for a in around], axis=0))
            mixed = mixed[: 2 * PAD] + mixed[2 * PAD :]
            up = xs[1, 1, rows, :].astype(F32)
            for px in range(2):
                first = up + jnp.maximum(mixed[PAD * px : PAD * (px + 1)], 0.0)
                first_s[px, rows, :] = first.astype(BF16)

    def heads(qy, brick):
        for px in range(2):
            first = first_s[px]
            second = first.astype(F32) + jnp.maximum(dot(depth_w, first), 0.0)
            second_s[depth * PAD * px : depth * PAD * (px + 1), :] = second.astype(BF16)
        affinity = jax.nn.sigmoid(dot(head, second_s[...]))
        both = jnp.concatenate(split(affinity), axis=0)
        stacked = jnp.concatenate([both[:, block * i : block * (i + 1)] for i in range(4)], axis=0)
        if qy == 0:
            loads[0].wait()
        placed = dot(stacked, place[code // 2])
        for i in range(4):
            value = placed[48 * i : 48 * i + 24] + placed[48 * i + 24 : 48 * i + 48]
            for j in range(4):
                e = 4 * i + j
                brick[e, 0:24, :] = value[:, LANES * j : LANES * (j + 1)]
                tail = value[:, LANES * (4 + j) : LANES * (5 + j)]
                tail = sum(jnp.where(lane == 3 * qy + k, tail[8 * k : 8 * k + 8], 0.0) for k in range(3))
                if qy == 0:
                    br1[e, 24:32, :] = tail
                else:
                    br1[e, 24:32, :] = br1[e, 24:32, :] + tail

    def piece(qy, brick, v):
        b = inverse_s[0, v]
        i = lax.rem(b // 4 - anchor + brick_rows, brick_rows)
        valid = (i < 4).astype(F32)
        i = jnp.minimum(i, 3)
        j = lax.rem(b, 4)
        source = jnp.where(fy == 1, 3 - i, i)
        window = win[4 * i + j]
        part = window[8 * qy : 8 * qy + 8]
        window = jnp.concatenate([part] * 3 + ([window[16:24]] if qy else []), axis=0)
        return brick[4 * source + j] * window * valid

    def pair_start(qy, brick, pair_out, pair_in, kept):
        for t in range(chips):
            pair_out[t] = piece(qy, brick, 2 * t + 1 - core)
        copy = pltpu.make_async_remote_copy(
            src_ref=pair_out, dst_ref=pair_in, send_sem=pair_send.at[qy], recv_sem=pair_recv.at[qy],
            device_id={"patch": partner}, device_id_type=MESH,
        )
        copy.start()
        for t in range(chips):
            kept[t] = piece(qy, brick, 2 * t + core)
        return copy

    def cross_start(qy, copy, pair_in, kept, cross_out, cross_in):
        copy.wait()
        copies = []
        for off in range(1, chips):
            t = lax.rem(chip + off, chips)
            cross_out[off - 1] = kept[t] + pair_in[t]
            copies.append(
                pltpu.make_async_remote_copy(
                    src_ref=cross_out.at[off - 1], dst_ref=cross_in.at[off - 1],
                    send_sem=cross_send.at[qy, off - 1], recv_sem=cross_recv.at[qy, off - 1],
                    device_id={"patch": 2 * t + core}, device_id_type=MESH,
                )
            )
            copies[-1].start()
        return copies

    def cross_end(copies, pair_in, kept, cross_in):
        total = kept[chip] + pair_in[chip]
        for at, copy in enumerate(copies):
            copy.wait()
            total = total + cross_in[at]
        return total

    planes(0)
    for tell in tells:
        tell.wait()
    lane1 = lax.broadcasted_iota(jnp.int32, (1, LANES), 1)
    inverse_v[...] = sum(jnp.where(heard[d, 0:1, :] == lane1, d, 0) for d in range(n))
    fetch = pltpu.make_async_copy(inverse_v, inverse_s, inverse_sem)
    fetch.start()
    heads(0, br0)
    fetch.wait()
    loads[1].wait()
    pair0 = pair_start(0, br0, pair_out0, pair_in0, kept0)
    planes(1)
    cross0 = cross_start(0, pair0, pair_in0, kept0, cross_out0, cross_in0)
    heads(1, br1)
    pair1 = pair_start(1, br1, pair_out1, pair_in1, kept1)
    cross1 = cross_start(1, pair1, pair_in1, kept1, cross_out1, cross_in1)

    loads[2].wait()
    loads[3].wait()
    mine = inverse_s[0, me]
    window = jnp.zeros((1, win_out.shape[2]), F32)
    for i in range(4):
        count = jnp.zeros((1, LANES), F32)
        for d in range(n):
            at = mine // 4 - heard[d, 1:2, :]
            at = jnp.where(at < 0, at + brick_rows, at)
            count = count + jnp.where(at == i, 1.0, 0.0)
        window = window + count[:, 0:1] * win_out[4 * i + lax.rem(mine, 4)]
    out[0, 3:4, :] = window

    totals = (
        cross_end(cross0, pair_in0, kept0, cross_in0),
        cross_end(cross1, pair_in1, kept1, cross_in1),
    )
    tail = totals[1][24:32]
    right_px = lax.broadcasted_iota(jnp.int32, (24, LANES), 0) // 4 % 2 == 1
    result = jnp.zeros((24, fine), F32)
    for py in range(2):
        main = totals[py][0:24]
        tails = jnp.concatenate([jnp.where(lane == 3 * py + k, tail, 0.0) for k in range(3)], axis=0)
        wide = jnp.concatenate(
            [
                jnp.where(right_px, 0.0, main), jnp.where(right_px, main, 0.0),
                jnp.where(right_px, 0.0, tails), jnp.where(right_px, tails, 0.0),
            ],
            axis=1,
        )
        both = dot(jnp.concatenate(split(wide), axis=0), spread[py])
        result = result + (both[:24] + both[24:])
    for k in range(3):
        for z in range(depth):
            row = 8 * k + z
            out[0, k : k + 1, fine * z : fine * (z + 1)] = result[row : row + 1] + result[row + 4 : row + 5]


def on_device(features, w_in, w_plane, w_depth, w_head, brick_owner, patch_anchor, aug_code):
    n = lax.axis_size("patch")
    _, cin, depth, plane = features.shape
    half = math.isqrt(plane)
    block = plane // 4
    chips = n // 2
    place, spread, win, win_out = tables(half, depth)
    vmem = pl.BlockSpec(memory_space=pltpu.VMEM)
    smem = pl.BlockSpec(memory_space=pltpu.SMEM)
    hbm = pl.BlockSpec(memory_space=pl.ANY)
    rows = depth * PAD
    V = pltpu.VMEM
    dma = pltpu.SemaphoreType.DMA
    exchange = []
    for height in (24, 32):
        exchange += [V((chips, height, LANES), F32)] * 3 + [V((chips - 1, height, LANES), F32)] * 2
    return pl.pallas_call(
        functools.partial(kernel, n, half),
        out_shape=jax.ShapeDtypeStruct((1, 4, plane), F32),
        in_specs=[vmem] * 5 + [smem] * 3 + [hbm] * 4,
        out_specs=vmem,
        scratch_shapes=[
            V(place.shape, BF16), V(spread.shape, BF16), V(win.shape, F32), V(win_out.shape, F32), dma((4,)),
            V((rows, cin * depth), F32), V((2, 2 * PAD, 6 * PAD), F32), V((rows, rows), F32), V((3, 2 * rows), F32),
            V((3, 3, rows, plane), BF16), V((2, rows, plane), BF16), V((2 * rows, plane), BF16),
            V((16, 24, LANES), F32), V((16, 32, LANES), F32),
            V((2, LANES), jnp.int32), V((n, 2, LANES), jnp.int32), V((1, LANES), jnp.int32),
            pltpu.SMEM((1, LANES), jnp.int32), dma, dma((n - 1,)), dma((n - 1,)),
            *exchange,
            dma((2,)), dma((2,)), dma((2, chips - 1)), dma((2, chips - 1)),
        ],
        compiler_params=pltpu.CompilerParams(
            collective_id=0, has_side_effects=True, vmem_limit_bytes=48 * 1024 * 1024
        ),
        cost_estimate=pl.CostEstimate(flops=6_000_000_000, bytes_accessed=8_000_000, transcendentals=110_592),
    )(features, w_in, w_plane, w_depth, w_head, brick_owner, patch_anchor, aug_code, place, spread, win, win_out)


def solution(mesh):
    in_specs = (
        P(("group", "patch"), None, None, None),
        P(),
        P(),
        P(),
        P(),
        P(("group", "patch")),
        P(("group", "patch")),
        P(("group", "patch")),
    )
    out_specs = P(("group", "patch"), None, None)
    return jax.shard_map(
        on_device, mesh=mesh, in_specs=in_specs, out_specs=out_specs, check_vma=False
    )
```

```python
import functools
import math

import jax
import jax.numpy as jnp
import numpy as np
from jax import lax
from jax.experimental import pallas as pl
from jax.experimental.pallas import tpu as pltpu
from jax.sharding import PartitionSpec as P

MESH = pl.DeviceIdType.MESH
LANES = 128
TILE = 256
PAD = 32
F32 = jnp.float32
BF16 = jnp.bfloat16


def bump(length):
    position = (np.arange(length) + 0.5) / length
    return 0.1 + np.sin(np.pi * position) ** 2


def tables(half, depth):
    hb = half // 4
    cells = hb * hb
    rest = cells - LANES
    block = hb * half
    side = 2 * half
    fine = 4 * cells
    yc, xc = np.divmod(np.arange(cells), hb)
    groups = LANES // rest
    place = np.zeros((4, block, 8 * LANES), np.float32)
    for flip in range(4):
        fy, fx = flip % 2, flip // 2
        for j in range(4):
            ys = hb - 1 - yc if fy else yc
            xs = half - 1 - (hb * j + xc) if fx else hb * j + xc
            lane = ys * half + xs
            m = np.arange(LANES)
            place[flip, lane[:LANES], j * LANES + m] = 1
            for g in range(groups):
                place[flip, lane[LANES:], (4 + j) * LANES + rest * g + np.arange(rest)] = 1
    spread = np.zeros((2, 4 * LANES, fine), np.float32)
    for py in range(2):
        for px in range(2):
            cell = (2 * yc + py) * (2 * hb) + 2 * xc + px
            spread[py, px * LANES + np.arange(LANES), cell[:LANES]] = 1
            for g in range(groups):
                spread[py, (2 + px) * LANES + rest * g + np.arange(rest), cell[LANES:]] = 1
    bz, by = bump(depth), bump(side)
    win = np.zeros((16, 24, LANES), np.float32)
    win_out = np.zeros((16, 1, depth * fine), np.float32)
    for i in range(4):
        for j in range(4):
            rows = by[2 * hb * i : 2 * hb * (i + 1)]
            cols = by[2 * hb * j : 2 * hb * (j + 1)]
            win_out[i * 4 + j, 0] = (bz[:, None, None] * rows[None, :, None] * cols[None, None, :]).reshape(-1)
            for py in range(2):
                for px in range(2):
                    value = bz[:, None] * (rows[2 * yc + py] * cols[2 * xc + px])[None]
                    win[i * 4 + j, 8 * py + px * 4 : 8 * py + px * 4 + 4] = value[:, :LANES]
                    for k in range(3):
                        at = rest * (3 * py + k)
                        win[i * 4 + j, 16 + px * 4 : 20 + px * 4, at : at + rest] = value[:, LANES:]
    return (
        jnp.asarray(place, BF16),
        jnp.asarray(spread, BF16),
        jnp.asarray(win, F32),
        jnp.asarray(win_out, F32),
    )


def shifted(values, offset):
    rows, length = values.shape
    zeros = jnp.zeros((rows, abs(offset)), values.dtype)
    if offset > 0:
        return jnp.concatenate([values[:, offset:], zeros], axis=1)
    return jnp.concatenate([zeros, values[:, : length + offset]], axis=1)


def dot(a, b):
    return jnp.dot(a, b, preferred_element_type=F32)


def split(values):
    high = values.astype(BF16)
    return high, (values - high.astype(F32)).astype(BF16)


def kernel(
    n, half,
    feat_h, w_in_h, w_plane_h, w_depth_h, w_head_h, owner_h, anchor_h, code_h, place_h, spread_h, win_h, win_out_h,
    out,
    feat, w_in, w_plane, w_depth, w_head, owner_s, anchor_s, code_s, arg_sem,
    place, spread, win, win_out, table_sem,
    wi_s, wp_s, wd_s, wh_s, xs, first_s, second_s, br0, br1,
    say, heard, inverse_v, inverse_s, inverse_sem, say_sem, hear_sem,
    pair_out0, pair_in0, kept0, cross_out0, cross_in0,
    pair_out1, pair_in1, kept1, cross_out1, cross_in1,
    pair_send, pair_recv, cross_send, cross_recv,
):
    hidden = w_in.shape[0]
    cin = w_in.shape[1]
    depth = feat.shape[2]
    plane = half * half
    block = plane // 4
    chips = n // 2
    brick_rows = n // 4
    rest = plane // 16 - LANES
    fine = plane // 4
    me = lax.axis_index("patch")
    chip, core = me // 2, lax.rem(me, 2)
    partner = me + 1 - 2 * core
    tiles = [slice(at, at + TILE) for at in range(0, plane, TILE)]

    arguments = [
        pltpu.make_async_copy(h, v, arg_sem.at[s])
        for s, (h, v) in enumerate(
            (
                (owner_h, owner_s), (anchor_h, anchor_s), (code_h, code_s), (w_in_h, w_in),
                (w_plane_h, w_plane), (w_depth_h, w_depth), (w_head_h, w_head), (feat_h, feat),
            )
        )
    ]
    for argument in arguments:
        argument.start()
    loads = [
        pltpu.make_async_copy(h, v, table_sem.at[s])
        for s, (h, v) in enumerate(((place_h, place), (win_h, win), (spread_h, spread), (win_out_h, win_out)))
    ]
    for load in loads:
        load.start()

    barrier = pltpu.get_barrier_semaphore()
    for off in range(1, n):
        pl.semaphore_signal(barrier, inc=1, device_id={"patch": lax.rem(me + off, n)}, device_id_type=MESH)

    for argument in arguments[:7]:
        argument.wait()
    code = code_s[0]
    anchor = anchor_s[0]
    fz, fy, fx = code % 2, (code // 2) % 2, code // 4
    word = jnp.concatenate(
        [jnp.full((1, LANES), owner_s[0], jnp.int32), jnp.full((1, LANES), anchor, jnp.int32)], axis=0
    )
    say[...] = word
    heard[me] = word

    spread_cols = lax.broadcasted_iota(jnp.int32, (cin, cin * depth), 1) // depth
    spread_rows = lax.broadcasted_iota(jnp.int32, (cin, cin * depth), 0)
    wi_all = dot(w_in[...], (spread_cols == spread_rows).astype(F32).astype(BF16))
    section = lax.broadcasted_iota(jnp.int32, (hidden, cin * depth), 1) % depth
    wi_s[...] = jnp.zeros_like(wi_s)
    for z in range(depth):
        wi_s[PAD * z : PAD * z + hidden, :] = jnp.where(section == z, wi_all, 0.0)
    wp_s[...] = jnp.zeros_like(wp_s)
    taps = [w_plane[t].astype(F32) for t in range(9)]
    halves = (((0,), (1, 2)), ((0, 1), (2,)))
    for sy in range(2):
        for dyi in range(2):
            for px in range(2):
                for at, txs in enumerate(halves[px]):
                    total = sum(taps[3 * ty + tx] for ty in halves[sy][dyi] for tx in txs)
                    col = PAD * (3 * dyi + px + at)
                    wp_s[sy, PAD * px : PAD * px + hidden, col : col + hidden] = total
    wd_s[...] = jnp.zeros_like(wd_s)
    for z in range(2 * depth):
        for tz in range(3):
            if (z + tz - 1) // depth == z // depth:
                col = PAD * (z + tz - 1)
                wd_s[PAD * z : PAD * z + hidden, col : col + hidden] = w_depth[tz].astype(F32)
    wh_s[...] = jnp.zeros_like(wh_s)
    for m in range(2 * depth):
        wh_s[:, PAD * m : PAD * m + hidden] = w_head[...].astype(F32)
    row8 = lax.broadcasted_iota(jnp.int32, (8, 2 * depth * PAD), 0)
    col8 = lax.broadcasted_iota(jnp.int32, (8, 2 * depth * PAD), 1) // PAD
    z_from = jnp.where(fz == 1, depth - 1 - col8 % depth, col8 % depth)
    px_from = jnp.where(fx == 1, 1 - col8 // depth, col8 // depth)
    wanted = row8 == px_from * depth + z_from
    head = jnp.concatenate(
        [jnp.where(wanted, jnp.broadcast_to(wh_s[k : k + 1, :], wanted.shape), 0.0) for k in range(3)], axis=0
    ).astype(BF16)
    depth_w = wd_s[...].astype(BF16)

    project = wi_s[...].astype(BF16)
    arguments[7].wait()
    parts = []
    for cols in tiles:
        parts.append(dot(project, feat[0, :, :, cols].reshape(cin * depth, TILE)).astype(BF16))
    x = jnp.concatenate(parts, axis=1)
    lane_x = lax.broadcasted_iota(jnp.int32, (1, plane), 1) % half
    left = shifted(x, -1) * (lane_x >= 1).astype(F32).astype(BF16)
    right = shifted(x, 1) * (lane_x <= half - 2).astype(F32).astype(BF16)
    for dx, values in enumerate((left, x, right)):
        xs[0, dx] = shifted(values, -half)
        xs[1, dx] = values
        xs[2, dx] = shifted(values, half)

    pl.semaphore_wait(barrier, n - 1)
    tells = []
    for off in range(1, n):
        tells.append(
            pltpu.make_async_remote_copy(
                src_ref=say, dst_ref=heard.at[me], send_sem=say_sem.at[off - 1], recv_sem=hear_sem.at[off - 1],
                device_id={"patch": lax.rem(me + off, n)}, device_id_type=MESH,
            )
        )
        tells[-1].start()

    lane = lax.broadcasted_iota(jnp.int32, (8, LANES), 1) // rest

    def planes(qy):
        sy = jnp.where(fy == 1, 1 - qy, qy)
        w_high, w_low = split(wp_s[sy])
        weights = jnp.concatenate([w_high, w_low], axis=0)
        for cols in tiles:
            for z in range(depth):
                rows = slice(PAD * z, PAD * (z + 1))
                around = [xs[sy + dyi, dx, rows, cols] for dyi in range(2) for dx in range(3)]
                mixed = dot(weights, jnp.concatenate(around, axis=0))
                mixed = mixed[: 2 * PAD] + mixed[2 * PAD :]
                up = xs[1, 1, rows, cols].astype(F32)
                for px in range(2):
                    first = up + jnp.maximum(mixed[PAD * px : PAD * (px + 1)], 0.0)
                    at = PAD * (depth * px + z)
                    first_s[at : at + PAD, cols] = first.astype(BF16)

    def heads(qy, brick):
        for cols in tiles:
            first = first_s[:, cols]
            second = first.astype(F32) + jnp.maximum(dot(depth_w, first), 0.0)
            second_s[:, cols] = second.astype(BF16)
        both = []
        for cols in tiles:
            affinity = jax.nn.sigmoid(dot(head, second_s[:, cols]))
            both.append(jnp.concatenate(split(affinity), axis=0))
        both = jnp.concatenate(both, axis=1)
        stacked = jnp.concatenate([both[:, block * i : block * (i + 1)] for i in range(4)], axis=0)
        if qy == 0:
            loads[0].wait()
        placed = dot(stacked, place[code // 2])
        for i in range(4):
            value = placed[48 * i : 48 * i + 24] + placed[48 * i + 24 : 48 * i + 48]
            for j in range(4):
                e = 4 * i + j
                brick[e, 0:24, :] = value[:, LANES * j : LANES * (j + 1)]
                tail = value[:, LANES * (4 + j) : LANES * (5 + j)]
                tail = sum(jnp.where(lane == 3 * qy + k, tail[8 * k : 8 * k + 8], 0.0) for k in range(3))
                if qy == 0:
                    br1[e, 24:32, :] = tail
                else:
                    br1[e, 24:32, :] = br1[e, 24:32, :] + tail

    def piece(qy, brick, v):
        b = inverse_s[0, v]
        i = lax.rem(b // 4 - anchor + brick_rows, brick_rows)
        valid = (i < 4).astype(F32)
        i = jnp.minimum(i, 3)
        j = lax.rem(b, 4)
        source = jnp.where(fy == 1, 3 - i, i)
        window = win[4 * i + j]
        part = window[8 * qy : 8 * qy + 8]
        window = jnp.concatenate([part] * 3 + ([window[16:24]] if qy else []), axis=0)
        return brick[4 * source + j] * window * valid

    def pair_start(qy, brick, pair_out, pair_in, kept):
        for t in range(chips):
            pair_out[t] = piece(qy, brick, 2 * t + 1 - core)
        copy = pltpu.make_async_remote_copy(
            src_ref=pair_out, dst_ref=pair_in, send_sem=pair_send.at[qy], recv_sem=pair_recv.at[qy],
            device_id={"patch": partner}, device_id_type=MESH,
        )
        copy.start()
        for t in range(chips):
            kept[t] = piece(qy, brick, 2 * t + core)
        return copy

    def cross_start(qy, copy, pair_in, kept, cross_out, cross_in):
        copy.wait()
        copies = []
        for off in range(1, chips):
            t = lax.rem(chip + off, chips)
            cross_out[off - 1] = kept[t] + pair_in[t]
            copies.append(
                pltpu.make_async_remote_copy(
                    src_ref=cross_out.at[off - 1], dst_ref=cross_in.at[off - 1],
                    send_sem=cross_send.at[qy, off - 1], recv_sem=cross_recv.at[qy, off - 1],
                    device_id={"patch": 2 * t + core}, device_id_type=MESH,
                )
            )
            copies[-1].start()
        return copies

    def cross_end(copies, pair_in, kept, cross_in):
        total = kept[chip] + pair_in[chip]
        for at, copy in enumerate(copies):
            copy.wait()
            total = total + cross_in[at]
        return total

    planes(0)
    for tell in tells:
        tell.wait()
    lane1 = lax.broadcasted_iota(jnp.int32, (1, LANES), 1)
    inverse_v[...] = sum(jnp.where(heard[d, 0:1, :] == lane1, d, 0) for d in range(n))
    fetch = pltpu.make_async_copy(inverse_v, inverse_s, inverse_sem)
    fetch.start()
    heads(0, br0)
    fetch.wait()
    loads[1].wait()
    pair0 = pair_start(0, br0, pair_out0, pair_in0, kept0)
    planes(1)
    cross0 = cross_start(0, pair0, pair_in0, kept0, cross_out0, cross_in0)
    heads(1, br1)
    pair1 = pair_start(1, br1, pair_out1, pair_in1, kept1)
    cross1 = cross_start(1, pair1, pair_in1, kept1, cross_out1, cross_in1)

    loads[2].wait()
    loads[3].wait()
    mine = inverse_s[0, me]
    window = jnp.zeros((1, win_out.shape[2]), F32)
    for i in range(4):
        count = jnp.zeros((1, LANES), F32)
        for d in range(n):
            at = mine // 4 - heard[d, 1:2, :]
            at = jnp.where(at < 0, at + brick_rows, at)
            count = count + jnp.where(at == i, 1.0, 0.0)
        window = window + count[:, 0:1] * win_out[4 * i + lax.rem(mine, 4)]
    out[0, 3:4, :] = window

    totals = (
        cross_end(cross0, pair_in0, kept0, cross_in0),
        cross_end(cross1, pair_in1, kept1, cross_in1),
    )
    tail = totals[1][24:32]
    right_px = lax.broadcasted_iota(jnp.int32, (24, LANES), 0) // 4 % 2 == 1
    result = jnp.zeros((24, fine), F32)
    for py in range(2):
        main = totals[py][0:24]
        tails = jnp.concatenate([jnp.where(lane == 3 * py + k, tail, 0.0) for k in range(3)], axis=0)
        wide = jnp.concatenate(
            [
                jnp.where(right_px, 0.0, main), jnp.where(right_px, main, 0.0),
                jnp.where(right_px, 0.0, tails), jnp.where(right_px, tails, 0.0),
            ],
            axis=1,
        )
        both = dot(jnp.concatenate(split(wide), axis=0), spread[py])
        result = result + (both[:24] + both[24:])
    for k in range(3):
        for z in range(depth):
            row = 8 * k + z
            out[0, k : k + 1, fine * z : fine * (z + 1)] = result[row : row + 1] + result[row + 4 : row + 5]


def on_device(features, w_in, w_plane, w_depth, w_head, brick_owner, patch_anchor, aug_code):
    n = lax.axis_size("patch")
    _, cin, depth, plane = features.shape
    half = math.isqrt(plane)
    block = plane // 4
    chips = n // 2
    place, spread, win, win_out = tables(half, depth)
    vmem = pl.BlockSpec(memory_space=pltpu.VMEM)
    hbm = pl.BlockSpec(memory_space=pl.ANY)
    rows = depth * PAD
    V = pltpu.VMEM
    dma = pltpu.SemaphoreType.DMA
    exchange = []
    for height in (24, 32):
        exchange += [V((chips, height, LANES), F32)] * 3 + [V((chips - 1, height, LANES), F32)] * 2
    return pl.pallas_call(
        functools.partial(kernel, n, half),
        out_shape=jax.ShapeDtypeStruct((1, 4, plane), F32),
        in_specs=[hbm] * 12,
        out_specs=vmem,
        scratch_shapes=[
            V(features.shape, BF16), V(w_in.shape, BF16), V(w_plane.shape, BF16), V(w_depth.shape, BF16),
            V(w_head.shape, BF16), *[pltpu.SMEM((1,), jnp.int32)] * 3, dma((8,)),
            V(place.shape, BF16), V(spread.shape, BF16), V(win.shape, F32), V(win_out.shape, F32), dma((4,)),
            V((rows, cin * depth), F32), V((2, 2 * PAD, 6 * PAD), F32), V((2 * rows, 2 * rows), F32), V((3, 2 * rows), F32),
            V((3, 3, rows, plane), BF16), V((2 * rows, plane), BF16), V((2 * rows, plane), BF16),
            V((16, 24, LANES), F32), V((16, 32, LANES), F32),
            V((2, LANES), jnp.int32), V((n, 2, LANES), jnp.int32), V((1, LANES), jnp.int32),
            pltpu.SMEM((1, LANES), jnp.int32), dma, dma((n - 1,)), dma((n - 1,)),
            *exchange,
            dma((2,)), dma((2,)), dma((2, chips - 1)), dma((2, chips - 1)),
        ],
        compiler_params=pltpu.CompilerParams(
            collective_id=0, has_side_effects=True, vmem_limit_bytes=48 * 1024 * 1024
        ),
        cost_estimate=pl.CostEstimate(flops=6_000_000_000, bytes_accessed=8_000_000, transcendentals=110_592),
    )(features, w_in, w_plane, w_depth, w_head, brick_owner, patch_anchor, aug_code, place, spread, win, win_out)


def solution(mesh):
    in_specs = (
        P(("group", "patch"), None, None, None),
        P(),
        P(),
        P(),
        P(),
        P(("group", "patch")),
        P(("group", "patch")),
        P(("group", "patch")),
    )
    out_specs = P(("group", "patch"), None, None)
    return jax.shard_map(
        on_device, mesh=mesh, in_specs=in_specs, out_specs=out_specs, check_vma=False
    )
```

```python
import functools
import math

import jax
import jax.numpy as jnp
import numpy as np
from jax import lax
from jax.experimental import pallas as pl
from jax.experimental.pallas import tpu as pltpu
from jax.sharding import PartitionSpec as P

MESH = pl.DeviceIdType.MESH
LANES = 128
TILE = 256
PAD = 32
F32 = jnp.float32
BF16 = jnp.bfloat16


def bump(length):
    position = (np.arange(length) + 0.5) / length
    return 0.1 + np.sin(np.pi * position) ** 2


def tables(half, depth):
    hb = half // 4
    cells = hb * hb
    rest = cells - LANES
    block = hb * half
    side = 2 * half
    fine = 4 * cells
    yc, xc = np.divmod(np.arange(cells), hb)
    groups = LANES // rest
    place = np.zeros((4, block, 8 * LANES), np.float32)
    for flip in range(4):
        fy, fx = flip % 2, flip // 2
        for j in range(4):
            ys = hb - 1 - yc if fy else yc
            xs = half - 1 - (hb * j + xc) if fx else hb * j + xc
            lane = ys * half + xs
            m = np.arange(LANES)
            place[flip, lane[:LANES], j * LANES + m] = 1
            for g in range(groups):
                place[flip, lane[LANES:], (4 + j) * LANES + rest * g + np.arange(rest)] = 1
    spread = np.zeros((2, 4 * LANES, fine), np.float32)
    for py in range(2):
        for px in range(2):
            cell = (2 * yc + py) * (2 * hb) + 2 * xc + px
            spread[py, px * LANES + np.arange(LANES), cell[:LANES]] = 1
            for g in range(groups):
                spread[py, (2 + px) * LANES + rest * g + np.arange(rest), cell[LANES:]] = 1
    bz, by = bump(depth), bump(side)
    win = np.zeros((17, 24, LANES), np.float32)
    win_out = np.zeros((16, 1, depth * fine), np.float32)
    for i in range(4):
        for j in range(4):
            rows = by[2 * hb * i : 2 * hb * (i + 1)]
            cols = by[2 * hb * j : 2 * hb * (j + 1)]
            win_out[i * 4 + j, 0] = (bz[:, None, None] * rows[None, :, None] * cols[None, None, :]).reshape(-1)
            for py in range(2):
                for px in range(2):
                    value = bz[:, None] * (rows[2 * yc + py] * cols[2 * xc + px])[None]
                    win[i * 4 + j, 8 * py + px * 4 : 8 * py + px * 4 + 4] = value[:, :LANES]
                    for k in range(3):
                        at = rest * (3 * py + k)
                        win[i * 4 + j, 16 + px * 4 : 20 + px * 4, at : at + rest] = value[:, LANES:]
    return (
        jnp.asarray(place, BF16),
        jnp.asarray(spread, BF16),
        jnp.asarray(win, F32),
        jnp.asarray(win_out, F32),
    )


def shifted(values, offset):
    rows, length = values.shape
    zeros = jnp.zeros((rows, abs(offset)), values.dtype)
    if offset > 0:
        return jnp.concatenate([values[:, offset:], zeros], axis=1)
    return jnp.concatenate([zeros, values[:, : length + offset]], axis=1)


def dot(a, b):
    return jnp.dot(a, b, preferred_element_type=F32)


def split(values):
    high = values.astype(BF16)
    return high, (values - high.astype(F32)).astype(BF16)


def kernel(
    n, half,
    feat_h, w_in_h, w_plane_h, w_depth_h, w_head_h, owner_h, anchor_h, code_h, place_h, spread_h, win_h, win_out_h,
    out,
    feat, w_in, w_plane, w_depth, w_head, owner_s, anchor_s, code_s, arg_sem,
    place, spread, win, win_out, table_sem,
    wi_s, wp_s, wd_s, wh_s, xs, first_s, second_s, br0, br1,
    say, heard, inverse_v, inverse_s, inverse_sem, say_sem, hear_sem,
    pair_out0, pair_in0, kept0, cross_out0, cross_in0,
    pair_out1, pair_in1, kept1, cross_out1, cross_in1,
    pair_send, pair_recv, cross_send, cross_recv,
):
    hidden = w_in.shape[0]
    cin = w_in.shape[1]
    depth = feat.shape[2]
    plane = half * half
    block = plane // 4
    chips = n // 2
    brick_rows = n // 4
    rest = plane // 16 - LANES
    fine = plane // 4
    me = lax.axis_index("patch")
    chip, core = me // 2, lax.rem(me, 2)
    partner = me + 1 - 2 * core
    tiles = [slice(at, at + TILE) for at in range(0, plane, TILE)]

    arguments = [
        pltpu.make_async_copy(h, v, arg_sem.at[s])
        for s, (h, v) in enumerate(
            (
                (owner_h, owner_s), (anchor_h, anchor_s), (code_h, code_s), (w_in_h, w_in),
                (w_plane_h, w_plane), (w_depth_h, w_depth), (w_head_h, w_head), (feat_h, feat),
            )
        )
    ]
    for argument in arguments:
        argument.start()
    loads = [
        pltpu.make_async_copy(h, v, table_sem.at[s])
        for s, (h, v) in enumerate(((place_h, place), (win_h, win), (spread_h, spread), (win_out_h, win_out)))
    ]
    barrier = pltpu.get_barrier_semaphore()
    for off in range(1, n):
        pl.semaphore_signal(barrier, inc=1, device_id={"patch": lax.rem(me + off, n)}, device_id_type=MESH)

    for argument in arguments[:7]:
        argument.wait()
    code = code_s[0]
    anchor = anchor_s[0]
    fz, fy, fx = code % 2, (code // 2) % 2, code // 4
    word = jnp.concatenate(
        [jnp.full((1, LANES), owner_s[0], jnp.int32), jnp.full((1, LANES), anchor, jnp.int32)], axis=0
    )
    say[...] = word
    heard[me] = word

    spread_cols = lax.broadcasted_iota(jnp.int32, (cin, cin * depth), 1) // depth
    spread_rows = lax.broadcasted_iota(jnp.int32, (cin, cin * depth), 0)
    wi_all = dot(w_in[...], (spread_cols == spread_rows).astype(F32).astype(BF16))
    section = lax.broadcasted_iota(jnp.int32, (hidden, cin * depth), 1) % depth
    wi_s[...] = jnp.zeros_like(wi_s)
    for z in range(depth):
        wi_s[PAD * z : PAD * z + hidden, :] = jnp.where(section == z, wi_all, 0.0)
    wp_s[...] = jnp.zeros_like(wp_s)
    taps = [w_plane[t].astype(F32) for t in range(9)]
    halves = (((0,), (1, 2)), ((0, 1), (2,)))
    for sy in range(2):
        for dyi in range(2):
            for px in range(2):
                for at, txs in enumerate(halves[px]):
                    total = sum(taps[3 * ty + tx] for ty in halves[sy][dyi] for tx in txs)
                    col = PAD * (3 * dyi + px + at)
                    wp_s[sy, PAD * px : PAD * px + hidden, col : col + hidden] = total
    wd_s[...] = jnp.zeros_like(wd_s)
    for z in range(2 * depth):
        for tz in range(3):
            if (z + tz - 1) // depth == z // depth:
                col = PAD * (z + tz - 1)
                wd_s[PAD * z : PAD * z + hidden, col : col + hidden] = w_depth[tz].astype(F32)
    wh_s[...] = jnp.zeros_like(wh_s)
    for m in range(2 * depth):
        wh_s[:, PAD * m : PAD * m + hidden] = w_head[...].astype(F32)
    row8 = lax.broadcasted_iota(jnp.int32, (8, 2 * depth * PAD), 0)
    col8 = lax.broadcasted_iota(jnp.int32, (8, 2 * depth * PAD), 1) // PAD
    z_from = jnp.where(fz == 1, depth - 1 - col8 % depth, col8 % depth)
    px_from = jnp.where(fx == 1, 1 - col8 // depth, col8 // depth)
    wanted = row8 == px_from * depth + z_from
    head = jnp.concatenate(
        [jnp.where(wanted, jnp.broadcast_to(wh_s[k : k + 1, :], wanted.shape), 0.0) for k in range(3)], axis=0
    ).astype(BF16)
    depth_w = wd_s[...].astype(BF16)

    project = wi_s[...].astype(BF16)
    arguments[7].wait()
    for load in loads:
        load.start()
    parts = []
    for cols in tiles:
        parts.append(dot(project, feat[0, :, :, cols].reshape(cin * depth, TILE)).astype(BF16))
    x = jnp.concatenate(parts, axis=1)
    lane_x = lax.broadcasted_iota(jnp.int32, (1, plane), 1) % half
    left = shifted(x, -1) * (lane_x >= 1).astype(F32).astype(BF16)
    right = shifted(x, 1) * (lane_x <= half - 2).astype(F32).astype(BF16)
    for dx, values in enumerate((left, x, right)):
        xs[0, dx] = shifted(values, -half)
        xs[1, dx] = values
        xs[2, dx] = shifted(values, half)

    pl.semaphore_wait(barrier, n - 1)
    tells = []
    for off in range(1, n):
        tells.append(
            pltpu.make_async_remote_copy(
                src_ref=say, dst_ref=heard.at[me], send_sem=say_sem.at[off - 1], recv_sem=hear_sem.at[off - 1],
                device_id={"patch": lax.rem(me + off, n)}, device_id_type=MESH,
            )
        )
        tells[-1].start()

    lane = lax.broadcasted_iota(jnp.int32, (8, LANES), 1) // rest

    def planes(qy):
        sy = jnp.where(fy == 1, 1 - qy, qy)
        w_high, w_low = split(wp_s[sy])
        weights = jnp.concatenate([w_high, w_low], axis=0)
        for cols in tiles:
            for z in range(depth):
                rows = slice(PAD * z, PAD * (z + 1))
                around = [xs[sy + dyi, dx, rows, cols] for dyi in range(2) for dx in range(3)]
                mixed = dot(weights, jnp.concatenate(around, axis=0))
                mixed = mixed[: 2 * PAD] + mixed[2 * PAD :]
                up = xs[1, 1, rows, cols].astype(F32)
                for px in range(2):
                    first = up + jnp.maximum(mixed[PAD * px : PAD * (px + 1)], 0.0)
                    at = PAD * (depth * px + z)
                    first_s[at : at + PAD, cols] = first.astype(BF16)

    def heads(qy, brick):
        for cols in tiles:
            first = first_s[:, cols]
            second = first.astype(F32) + jnp.maximum(dot(depth_w, first), 0.0)
            second_s[:, cols] = second.astype(BF16)
        both = []
        for cols in tiles:
            affinity = jax.nn.sigmoid(dot(head, second_s[:, cols]))
            both.append(jnp.concatenate(split(affinity), axis=0))
        both = jnp.concatenate(both, axis=1)
        stacked = jnp.concatenate([both[:, block * i : block * (i + 1)] for i in range(4)], axis=0)
        if qy == 0:
            loads[0].wait()
        placed = dot(stacked, place[code // 2])
        for i in range(4):
            value = placed[48 * i : 48 * i + 24] + placed[48 * i + 24 : 48 * i + 48]
            for j in range(4):
                e = 4 * i + j
                brick[e, 0:24, :] = value[:, LANES * j : LANES * (j + 1)]
                tail = value[:, LANES * (4 + j) : LANES * (5 + j)]
                tail = sum(jnp.where(lane == 3 * qy + k, tail[8 * k : 8 * k + 8], 0.0) for k in range(3))
                if qy == 0:
                    br1[e, 24:32, :] = tail
                else:
                    br1[e, 24:32, :] = br1[e, 24:32, :] + tail

    def piece(qy, brick, v):
        window = win[inverse_s[2, v]]
        part = window[8 * qy : 8 * qy + 8]
        window = jnp.concatenate([part] * 3 + ([window[16:24]] if qy else []), axis=0)
        return brick[inverse_s[1, v]] * window

    cut = chips // 2
    spans = (slice(0, cut), slice(cut, chips))

    def pair_start(qy, brick, pair_out, pair_in, kept):
        copies = []
        for part, span in enumerate(spans):
            for slot in range(span.start, span.stop):
                pair_out[slot] = piece(qy, brick, 2 * lax.rem(chip + slot + 1, chips) + 1 - core)
            window = pl.ds(span.start, span.stop - span.start)
            copies.append(
                pltpu.make_async_remote_copy(
                    src_ref=pair_out.at[window], dst_ref=pair_in.at[window],
                    send_sem=pair_send.at[qy, part], recv_sem=pair_recv.at[qy, part],
                    device_id={"patch": partner}, device_id_type=MESH,
                )
            )
            copies[-1].start()
        for slot in range(chips):
            kept[slot] = piece(qy, brick, 2 * lax.rem(chip + slot + 1, chips) + core)
        return copies

    def cross_start(qy, pairs, pair_in, kept, cross_out, cross_in):
        copies = []
        for pair, span in zip(pairs, spans):
            pair.wait()
            for slot in range(span.start, min(span.stop, chips - 1)):
                cross_out[slot] = kept[slot] + pair_in[slot]
                copies.append(
                    pltpu.make_async_remote_copy(
                        src_ref=cross_out.at[slot], dst_ref=cross_in.at[slot],
                        send_sem=cross_send.at[qy, slot], recv_sem=cross_recv.at[qy, slot],
                        device_id={"patch": 2 * lax.rem(chip + slot + 1, chips) + core}, device_id_type=MESH,
                    )
                )
                copies[-1].start()
        return copies

    def cross_end(copies, pair_in, kept, cross_in):
        total = kept[chips - 1] + pair_in[chips - 1]
        for at, copy in enumerate(copies):
            copy.wait()
            total = total + cross_in[at]
        return total

    planes(0)
    for tell in tells:
        tell.wait()
    lane1 = lax.broadcasted_iota(jnp.int32, (1, LANES), 1)
    inverse = sum(jnp.where(heard[d, 0:1, :] == lane1, d, 0) for d in range(n))
    i = inverse // 4 - anchor
    i = jnp.where(i < 0, i + brick_rows, i)
    j = inverse % 4
    held_i = jnp.minimum(i, 3)
    inverse_v[0:1, :] = inverse
    inverse_v[1:2, :] = 4 * jnp.where(fy == 1, 3 - held_i, held_i) + j
    inverse_v[2:3, :] = jnp.where(i < 4, 4 * held_i + j, 16)
    inverse_v[3:8, :] = jnp.zeros((5, LANES), jnp.int32)
    fetch = pltpu.make_async_copy(inverse_v, inverse_s, inverse_sem)
    fetch.start()
    heads(0, br0)
    fetch.wait()
    loads[1].wait()
    pair0 = pair_start(0, br0, pair_out0, pair_in0, kept0)
    planes(1)
    cross0 = cross_start(0, pair0, pair_in0, kept0, cross_out0, cross_in0)
    heads(1, br1)
    pair1 = pair_start(1, br1, pair_out1, pair_in1, kept1)
    cross1 = cross_start(1, pair1, pair_in1, kept1, cross_out1, cross_in1)

    loads[2].wait()
    loads[3].wait()
    mine = inverse_s[0, me]
    window = jnp.zeros((1, win_out.shape[2]), F32)
    for i in range(4):
        count = jnp.zeros((1, LANES), F32)
        for d in range(n):
            at = mine // 4 - heard[d, 1:2, :]
            at = jnp.where(at < 0, at + brick_rows, at)
            count = count + jnp.where(at == i, 1.0, 0.0)
        window = window + count[:, 0:1] * win_out[4 * i + lax.rem(mine, 4)]
    out[0, 3:4, :] = window

    totals = (
        cross_end(cross0, pair_in0, kept0, cross_in0),
        cross_end(cross1, pair_in1, kept1, cross_in1),
    )
    tail = totals[1][24:32]
    right_px = lax.broadcasted_iota(jnp.int32, (24, LANES), 0) // 4 % 2 == 1
    result = jnp.zeros((24, fine), F32)
    for py in range(2):
        main = totals[py][0:24]
        tails = jnp.concatenate([jnp.where(lane == 3 * py + k, tail, 0.0) for k in range(3)], axis=0)
        wide = jnp.concatenate(
            [
                jnp.where(right_px, 0.0, main), jnp.where(right_px, main, 0.0),
                jnp.where(right_px, 0.0, tails), jnp.where(right_px, tails, 0.0),
            ],
            axis=1,
        )
        both = dot(jnp.concatenate(split(wide), axis=0), spread[py])
        result = result + (both[:24] + both[24:])
    for k in range(3):
        for z in range(depth):
            row = 8 * k + z
            out[0, k : k + 1, fine * z : fine * (z + 1)] = result[row : row + 1] + result[row + 4 : row + 5]


def on_device(features, w_in, w_plane, w_depth, w_head, brick_owner, patch_anchor, aug_code):
    n = lax.axis_size("patch")
    _, cin, depth, plane = features.shape
    half = math.isqrt(plane)
    block = plane // 4
    chips = n // 2
    place, spread, win, win_out = tables(half, depth)
    vmem = pl.BlockSpec(memory_space=pltpu.VMEM)
    hbm = pl.BlockSpec(memory_space=pltpu.HBM)
    rows = depth * PAD
    V = pltpu.VMEM
    dma = pltpu.SemaphoreType.DMA
    exchange = []
    for height in (24, 32):
        exchange += [V((chips, height, LANES), F32)] * 3 + [V((chips - 1, height, LANES), F32)] * 2
    return pl.pallas_call(
        functools.partial(kernel, n, half),
        out_shape=jax.ShapeDtypeStruct((1, 4, plane), F32),
        in_specs=[hbm] * 12,
        out_specs=vmem,
        scratch_shapes=[
            V(features.shape, BF16), V(w_in.shape, BF16), V(w_plane.shape, BF16), V(w_depth.shape, BF16),
            V(w_head.shape, BF16), *[pltpu.SMEM((1,), jnp.int32)] * 3, dma((8,)),
            V(place.shape, BF16), V(spread.shape, BF16), V(win.shape, F32), V(win_out.shape, F32), dma((4,)),
            V((rows, cin * depth), F32), V((2, 2 * PAD, 6 * PAD), F32), V((2 * rows, 2 * rows), F32), V((3, 2 * rows), F32),
            V((3, 3, rows, plane), BF16), V((2 * rows, plane), BF16), V((2 * rows, plane), BF16),
            V((16, 24, LANES), F32), V((16, 32, LANES), F32),
            V((2, LANES), jnp.int32), V((n, 2, LANES), jnp.int32), V((8, LANES), jnp.int32),
            pltpu.SMEM((8, LANES), jnp.int32), dma, dma((n - 1,)), dma((n - 1,)),
            *exchange,
            dma((2, 2)), dma((2, 2)), dma((2, chips - 1)), dma((2, chips - 1)),
        ],
        compiler_params=pltpu.CompilerParams(
            collective_id=0, has_side_effects=True, vmem_limit_bytes=60 * 1024 * 1024
        ),
        cost_estimate=pl.CostEstimate(flops=6_000_000_000, bytes_accessed=8_000_000, transcendentals=110_592),
    )(features, w_in, w_plane, w_depth, w_head, brick_owner, patch_anchor, aug_code, place, spread, win, win_out)


def solution(mesh):
    in_specs = (
        P(("group", "patch"), None, None, None),
        P(),
        P(),
        P(),
        P(),
        P(("group", "patch")),
        P(("group", "patch")),
        P(("group", "patch")),
    )
    out_specs = P(("group", "patch"), None, None)
    return jax.shard_map(
        on_device, mesh=mesh, in_specs=in_specs, out_specs=out_specs, check_vma=False
    )
```

```python
import functools
import math

import jax
import jax.numpy as jnp
import numpy as np
from jax import lax
from jax.experimental import pallas as pl
from jax.experimental.pallas import tpu as pltpu
from jax.sharding import PartitionSpec as P

MESH = pl.DeviceIdType.MESH
LANES = 128
TILE = 256
PAD = 32
F32 = jnp.float32
BF16 = jnp.bfloat16


def bump(length):
    position = (np.arange(length) + 0.5) / length
    return 0.1 + np.sin(np.pi * position) ** 2


def tables(half, depth):
    hb = half // 4
    cells = hb * hb
    rest = cells - LANES
    block = hb * half
    side = 2 * half
    fine = 4 * cells
    yc, xc = np.divmod(np.arange(cells), hb)
    groups = LANES // rest
    place = np.zeros((4, block, 8 * LANES), np.float32)
    for flip in range(4):
        fy, fx = flip % 2, flip // 2
        for j in range(4):
            ys = hb - 1 - yc if fy else yc
            xs = half - 1 - (hb * j + xc) if fx else hb * j + xc
            lane = ys * half + xs
            m = np.arange(LANES)
            place[flip, lane[:LANES], j * LANES + m] = 1
            for g in range(groups):
                place[flip, lane[LANES:], (4 + j) * LANES + rest * g + np.arange(rest)] = 1
    spread = np.zeros((2, 4 * LANES, fine), np.float32)
    for py in range(2):
        for px in range(2):
            cell = (2 * yc + py) * (2 * hb) + 2 * xc + px
            spread[py, px * LANES + np.arange(LANES), cell[:LANES]] = 1
            for g in range(groups):
                spread[py, (2 + px) * LANES + rest * g + np.arange(rest), cell[LANES:]] = 1
    bz, by = bump(depth), bump(side)
    win = np.zeros((17, 24, LANES), np.float32)
    win_out = np.zeros((16, 1, depth * fine), np.float32)
    for i in range(4):
        for j in range(4):
            rows = by[2 * hb * i : 2 * hb * (i + 1)]
            cols = by[2 * hb * j : 2 * hb * (j + 1)]
            win_out[i * 4 + j, 0] = (bz[:, None, None] * rows[None, :, None] * cols[None, None, :]).reshape(-1)
            for py in range(2):
                for px in range(2):
                    value = bz[:, None] * (rows[2 * yc + py] * cols[2 * xc + px])[None]
                    win[i * 4 + j, 8 * py + px * 4 : 8 * py + px * 4 + 4] = value[:, :LANES]
                    for k in range(3):
                        at = rest * (3 * py + k)
                        win[i * 4 + j, 16 + px * 4 : 20 + px * 4, at : at + rest] = value[:, LANES:]
    return (
        jnp.asarray(place, BF16),
        jnp.asarray(spread, BF16),
        jnp.asarray(win, F32),
        jnp.asarray(win_out, F32),
    )


def shifted(values, offset):
    rows, length = values.shape
    zeros = jnp.zeros((rows, abs(offset)), values.dtype)
    if offset > 0:
        return jnp.concatenate([values[:, offset:], zeros], axis=1)
    return jnp.concatenate([zeros, values[:, : length + offset]], axis=1)


def dot(a, b):
    return jnp.dot(a, b, preferred_element_type=F32)


def split(values):
    high = values.astype(BF16)
    return high, (values - high.astype(F32)).astype(BF16)


def kernel(
    n, half,
    feat_h, w_in_h, w_plane_h, w_depth_h, w_head_h, owner_h, anchor_h, code_h, place_h, spread_h, win_h, win_out_h,
    out,
    feat, w_in, w_plane, w_depth, w_head, owner_s, anchor_s, code_s, arg_sem,
    place, spread, win, win_out, table_sem,
    wi_s, wp_s, wd_s, wh_s, xs, first_s, second_s, br0, br1,
    say, heard, inverse_v, inverse_s, inverse_sem, say_sem, hear_sem,
    pair_out0, pair_in0, kept0, cross_out0, cross_in0,
    pair_out1, pair_in1, kept1, cross_out1, cross_in1,
    pair_send, pair_recv, cross_send, cross_recv,
):
    hidden = w_in.shape[0]
    cin = w_in.shape[1]
    depth = feat.shape[2]
    plane = half * half
    block = plane // 4
    chips = n // 2
    brick_rows = n // 4
    rest = plane // 16 - LANES
    fine = plane // 4
    me = lax.axis_index("patch")
    chip, core = me // 2, lax.rem(me, 2)
    partner = me + 1 - 2 * core
    tiles = [slice(at, at + TILE) for at in range(0, plane, TILE)]

    arguments = [
        pltpu.make_async_copy(h, v, arg_sem.at[s])
        for s, (h, v) in enumerate(
            (
                (owner_h, owner_s), (anchor_h, anchor_s), (code_h, code_s), (w_in_h, w_in),
                (w_plane_h, w_plane), (w_depth_h, w_depth), (w_head_h, w_head), (feat_h, feat),
            )
        )
    ]
    for argument in arguments:
        argument.start()
    loads = [
        pltpu.make_async_copy(h, v, table_sem.at[s])
        for s, (h, v) in enumerate(((place_h, place), (win_h, win), (spread_h, spread), (win_out_h, win_out)))
    ]
    barrier = pltpu.get_barrier_semaphore()
    for off in range(1, n):
        pl.semaphore_signal(barrier, inc=1, device_id={"patch": lax.rem(me + off, n)}, device_id_type=MESH)

    for argument in arguments:
        argument.wait()
    for load in loads:
        load.start()
    code = code_s[0]
    anchor = anchor_s[0]
    fz, fy, fx = code % 2, (code // 2) % 2, code // 4
    word = jnp.concatenate(
        [jnp.full((1, LANES), owner_s[0], jnp.int32), jnp.full((1, LANES), anchor, jnp.int32)], axis=0
    )
    say[...] = word
    heard[me] = word

    spread_cols = lax.broadcasted_iota(jnp.int32, (cin, cin * depth), 1) // depth
    spread_rows = lax.broadcasted_iota(jnp.int32, (cin, cin * depth), 0)
    wi_all = dot(w_in[...], (spread_cols == spread_rows).astype(F32).astype(BF16))
    section = lax.broadcasted_iota(jnp.int32, (hidden, cin * depth), 1) % depth
    wi_s[...] = jnp.zeros_like(wi_s)
    for z in range(depth):
        wi_s[PAD * z : PAD * z + hidden, :] = jnp.where(section == z, wi_all, 0.0)
    project = wi_s[...].astype(BF16)
    parts = []
    for cols in tiles:
        parts.append(dot(project, feat[0, :, :, cols].reshape(cin * depth, TILE)).astype(BF16))
    x = jnp.concatenate(parts, axis=1)
    lane_x = lax.broadcasted_iota(jnp.int32, (1, plane), 1) % half
    left = shifted(x, -1) * (lane_x >= 1).astype(F32).astype(BF16)
    right = shifted(x, 1) * (lane_x <= half - 2).astype(F32).astype(BF16)
    for dx, values in enumerate((left, x, right)):
        xs[0, dx] = shifted(values, -half)
        xs[1, dx] = values
        xs[2, dx] = shifted(values, half)

    wp_s[...] = jnp.zeros_like(wp_s)
    taps = [w_plane[t].astype(F32) for t in range(9)]
    halves = (((0,), (1, 2)), ((0, 1), (2,)))
    for sy in range(2):
        for dyi in range(2):
            for px in range(2):
                for at, txs in enumerate(halves[px]):
                    total = sum(taps[3 * ty + tx] for ty in halves[sy][dyi] for tx in txs)
                    col = PAD * (3 * dyi + px + at)
                    wp_s[sy, PAD * px : PAD * px + hidden, col : col + hidden] = total
    wd_s[...] = jnp.zeros_like(wd_s)
    for z in range(2 * depth):
        for tz in range(3):
            if (z + tz - 1) // depth == z // depth:
                col = PAD * (z + tz - 1)
                wd_s[PAD * z : PAD * z + hidden, col : col + hidden] = w_depth[tz].astype(F32)
    wh_s[...] = jnp.zeros_like(wh_s)
    for m in range(2 * depth):
        wh_s[:, PAD * m : PAD * m + hidden] = w_head[...].astype(F32)
    row8 = lax.broadcasted_iota(jnp.int32, (8, 2 * depth * PAD), 0)
    col8 = lax.broadcasted_iota(jnp.int32, (8, 2 * depth * PAD), 1) // PAD
    z_from = jnp.where(fz == 1, depth - 1 - col8 % depth, col8 % depth)
    px_from = jnp.where(fx == 1, 1 - col8 // depth, col8 // depth)
    wanted = row8 == px_from * depth + z_from
    head = jnp.concatenate(
        [jnp.where(wanted, jnp.broadcast_to(wh_s[k : k + 1, :], wanted.shape), 0.0) for k in range(3)], axis=0
    ).astype(BF16)
    depth_w = wd_s[...].astype(BF16)

    pl.semaphore_wait(barrier, n - 1)
    tells = []
    for off in range(1, n):
        tells.append(
            pltpu.make_async_remote_copy(
                src_ref=say, dst_ref=heard.at[me], send_sem=say_sem.at[off - 1], recv_sem=hear_sem.at[off - 1],
                device_id={"patch": lax.rem(me + off, n)}, device_id_type=MESH,
            )
        )
        tells[-1].start()

    lane = lax.broadcasted_iota(jnp.int32, (8, LANES), 1) // rest

    def planes(qy):
        sy = jnp.where(fy == 1, 1 - qy, qy)
        w_high, w_low = split(wp_s[sy])
        weights = jnp.concatenate([w_high, w_low], axis=0)
        for cols in tiles:
            for z in range(depth):
                rows = slice(PAD * z, PAD * (z + 1))
                around = [xs[sy + dyi, dx, rows, cols] for dyi in range(2) for dx in range(3)]
                mixed = dot(weights, jnp.concatenate(around, axis=0))
                mixed = mixed[: 2 * PAD] + mixed[2 * PAD :]
                up = xs[1, 1, rows, cols].astype(F32)
                for px in range(2):
                    first = up + jnp.maximum(mixed[PAD * px : PAD * (px + 1)], 0.0)
                    at = PAD * (depth * px + z)
                    first_s[at : at + PAD, cols] = first.astype(BF16)

    def heads(qy, brick):
        for cols in tiles:
            first = first_s[:, cols]
            second = first.astype(F32) + jnp.maximum(dot(depth_w, first), 0.0)
            second_s[:, cols] = second.astype(BF16)
        both = []
        for cols in tiles:
            affinity = jax.nn.sigmoid(dot(head, second_s[:, cols]))
            both.append(jnp.concatenate(split(affinity), axis=0))
        both = jnp.concatenate(both, axis=1)
        stacked = jnp.concatenate([both[:, block * i : block * (i + 1)] for i in range(4)], axis=0)
        if qy == 0:
            loads[0].wait()
        placed = dot(stacked, place[code // 2])
        for i in range(4):
            value = placed[48 * i : 48 * i + 24] + placed[48 * i + 24 : 48 * i + 48]
            for j in range(4):
                e = 4 * i + j
                brick[e, 0:24, :] = value[:, LANES * j : LANES * (j + 1)]
                tail = value[:, LANES * (4 + j) : LANES * (5 + j)]
                tail = sum(jnp.where(lane == 3 * qy + k, tail[8 * k : 8 * k + 8], 0.0) for k in range(3))
                if qy == 0:
                    br1[e, 24:32, :] = tail
                else:
                    br1[e, 24:32, :] = br1[e, 24:32, :] + tail

    def piece(qy, brick, v):
        window = win[inverse_s[2, v]]
        part = window[8 * qy : 8 * qy + 8]
        window = jnp.concatenate([part] * 3 + ([window[16:24]] if qy else []), axis=0)
        return brick[inverse_s[1, v]] * window

    cut = chips // 2
    spans = (slice(0, cut), slice(cut, chips))

    def pair_start(qy, brick, pair_out, pair_in, kept):
        copies = []
        for part, span in enumerate(spans):
            for slot in range(span.start, span.stop):
                pair_out[slot] = piece(qy, brick, 2 * lax.rem(chip + slot + 1, chips) + 1 - core)
            window = pl.ds(span.start, span.stop - span.start)
            copies.append(
                pltpu.make_async_remote_copy(
                    src_ref=pair_out.at[window], dst_ref=pair_in.at[window],
                    send_sem=pair_send.at[qy, part], recv_sem=pair_recv.at[qy, part],
                    device_id={"patch": partner}, device_id_type=MESH,
                )
            )
            copies[-1].start()
        for slot in range(chips):
            kept[slot] = piece(qy, brick, 2 * lax.rem(chip + slot + 1, chips) + core)
        return copies

    def cross_start(qy, pairs, pair_in, kept, cross_out, cross_in):
        copies = []
        for pair, span in zip(pairs, spans):
            pair.wait()
            for slot in range(span.start, min(span.stop, chips - 1)):
                cross_out[slot] = kept[slot] + pair_in[slot]
                copies.append(
                    pltpu.make_async_remote_copy(
                        src_ref=cross_out.at[slot], dst_ref=cross_in.at[slot],
                        send_sem=cross_send.at[qy, slot], recv_sem=cross_recv.at[qy, slot],
                        device_id={"patch": 2 * lax.rem(chip + slot + 1, chips) + core}, device_id_type=MESH,
                    )
                )
                copies[-1].start()
        return copies

    def cross_end(copies, pair_in, kept, cross_in):
        total = kept[chips - 1] + pair_in[chips - 1]
        for at, copy in enumerate(copies):
            copy.wait()
            total = total + cross_in[at]
        return total

    planes(0)
    for tell in tells:
        tell.wait()
    lane1 = lax.broadcasted_iota(jnp.int32, (1, LANES), 1)
    inverse = sum(jnp.where(heard[d, 0:1, :] == lane1, d, 0) for d in range(n))
    i = inverse // 4 - anchor
    i = jnp.where(i < 0, i + brick_rows, i)
    j = inverse % 4
    held_i = jnp.minimum(i, 3)
    inverse_v[0:1, :] = inverse
    inverse_v[1:2, :] = 4 * jnp.where(fy == 1, 3 - held_i, held_i) + j
    inverse_v[2:3, :] = jnp.where(i < 4, 4 * held_i + j, 16)
    inverse_v[3:8, :] = jnp.zeros((5, LANES), jnp.int32)
    fetch = pltpu.make_async_copy(inverse_v, inverse_s, inverse_sem)
    fetch.start()
    heads(0, br0)
    fetch.wait()
    loads[1].wait()
    pair0 = pair_start(0, br0, pair_out0, pair_in0, kept0)
    planes(1)
    cross0 = cross_start(0, pair0, pair_in0, kept0, cross_out0, cross_in0)
    heads(1, br1)
    pair1 = pair_start(1, br1, pair_out1, pair_in1, kept1)
    cross1 = cross_start(1, pair1, pair_in1, kept1, cross_out1, cross_in1)

    loads[2].wait()
    loads[3].wait()
    mine = inverse_s[0, me]
    window = jnp.zeros((1, win_out.shape[2]), F32)
    for i in range(4):
        count = jnp.zeros((1, LANES), F32)
        for d in range(n):
            at = mine // 4 - heard[d, 1:2, :]
            at = jnp.where(at < 0, at + brick_rows, at)
            count = count + jnp.where(at == i, 1.0, 0.0)
        window = window + count[:, 0:1] * win_out[4 * i + lax.rem(mine, 4)]
    out[0, 3:4, :] = window

    right_px = lax.broadcasted_iota(jnp.int32, (24, LANES), 0) // 4 % 2 == 1

    def by_px(values):
        return [jnp.where(right_px, 0.0, values), jnp.where(right_px, values, 0.0)]

    def put(values, spreading):
        both = dot(jnp.concatenate(split(jnp.concatenate(values, axis=1)), axis=0), spreading)
        return both[:24] + both[24:]

    result = put(by_px(cross_end(cross0, pair_in0, kept0, cross_in0)), spread[0, 0 : 2 * LANES, :])
    total = cross_end(cross1, pair_in1, kept1, cross_in1)
    tail = total[24:32]
    tails = [
        jnp.concatenate([jnp.where(lane == 3 * py + k, tail, 0.0) for k in range(3)], axis=0) for py in range(2)
    ]
    result = result + put(by_px(tails[0]), spread[0, 2 * LANES :, :])
    result = result + put(by_px(total[0:24]) + by_px(tails[1]), spread[1])
    for k in range(3):
        for z in range(depth):
            row = 8 * k + z
            out[0, k : k + 1, fine * z : fine * (z + 1)] = result[row : row + 1] + result[row + 4 : row + 5]


def on_device(features, w_in, w_plane, w_depth, w_head, brick_owner, patch_anchor, aug_code):
    n = lax.axis_size("patch")
    _, cin, depth, plane = features.shape
    half = math.isqrt(plane)
    block = plane // 4
    chips = n // 2
    place, spread, win, win_out = tables(half, depth)
    vmem = pl.BlockSpec(memory_space=pltpu.VMEM)
    hbm = pl.BlockSpec(memory_space=pltpu.HBM)
    rows = depth * PAD
    V = pltpu.VMEM
    dma = pltpu.SemaphoreType.DMA
    exchange = []
    for height in (24, 32):
        exchange += [V((chips, height, LANES), F32)] * 3 + [V((chips - 1, height, LANES), F32)] * 2
    return pl.pallas_call(
        functools.partial(kernel, n, half),
        out_shape=jax.ShapeDtypeStruct((1, 4, plane), F32),
        in_specs=[hbm] * 12,
        out_specs=vmem,
        scratch_shapes=[
            V(features.shape, BF16), V(w_in.shape, BF16), V(w_plane.shape, BF16), V(w_depth.shape, BF16),
            V(w_head.shape, BF16), *[pltpu.SMEM((1,), jnp.int32)] * 3, dma((8,)),
            V(place.shape, BF16), V(spread.shape, BF16), V(win.shape, F32), V(win_out.shape, F32), dma((4,)),
            V((rows, cin * depth), F32), V((2, 2 * PAD, 6 * PAD), F32), V((2 * rows, 2 * rows), F32), V((3, 2 * rows), F32),
            V((3, 3, rows, plane), BF16), V((2 * rows, plane), BF16), V((2 * rows, plane), BF16),
            V((16, 24, LANES), F32), V((16, 32, LANES), F32),
            V((2, LANES), jnp.int32), V((n, 2, LANES), jnp.int32), V((8, LANES), jnp.int32),
            pltpu.SMEM((8, LANES), jnp.int32), dma, dma((n - 1,)), dma((n - 1,)),
            *exchange,
            dma((2, 2)), dma((2, 2)), dma((2, chips - 1)), dma((2, chips - 1)),
        ],
        compiler_params=pltpu.CompilerParams(
            collective_id=0, has_side_effects=True, vmem_limit_bytes=60 * 1024 * 1024
        ),
        cost_estimate=pl.CostEstimate(flops=6_000_000_000, bytes_accessed=8_000_000, transcendentals=110_592),
    )(features, w_in, w_plane, w_depth, w_head, brick_owner, patch_anchor, aug_code, place, spread, win, win_out)


def solution(mesh):
    in_specs = (
        P(("group", "patch"), None, None, None),
        P(),
        P(),
        P(),
        P(),
        P(("group", "patch")),
        P(("group", "patch")),
        P(("group", "patch")),
    )
    out_specs = P(("group", "patch"), None, None)
    return jax.shard_map(
        on_device, mesh=mesh, in_specs=in_specs, out_specs=out_specs, check_vma=False
    )
```

```python
import functools
import math

import jax
import jax.numpy as jnp
import numpy as np
from jax import lax
from jax.experimental import pallas as pl
from jax.experimental.pallas import tpu as pltpu
from jax.sharding import PartitionSpec as P

MESH = pl.DeviceIdType.MESH
LANES = 128
TILE = 256
PAD = 32
F32 = jnp.float32
BF16 = jnp.bfloat16


def bump(length):
    position = (np.arange(length) + 0.5) / length
    return 0.1 + np.sin(np.pi * position) ** 2


def tables(half, depth):
    hb = half // 4
    cells = hb * hb
    rest = cells - LANES
    block = hb * half
    side = 2 * half
    fine = 4 * cells
    yc, xc = np.divmod(np.arange(cells), hb)
    groups = LANES // rest
    place = np.zeros((4, block, 8 * LANES), np.float32)
    for flip in range(4):
        fy, fx = flip % 2, flip // 2
        for j in range(4):
            ys = hb - 1 - yc if fy else yc
            xs = half - 1 - (hb * j + xc) if fx else hb * j + xc
            lane = ys * half + xs
            m = np.arange(LANES)
            place[flip, lane[:LANES], j * LANES + m] = 1
            for g in range(groups):
                place[flip, lane[LANES:], (4 + j) * LANES + rest * g + np.arange(rest)] = 1
    spread = np.zeros((2, 4 * LANES, fine), np.float32)
    for py in range(2):
        for px in range(2):
            cell = (2 * yc + py) * (2 * hb) + 2 * xc + px
            spread[py, px * LANES + np.arange(LANES), cell[:LANES]] = 1
            for g in range(groups):
                spread[py, (2 + px) * LANES + rest * g + np.arange(rest), cell[LANES:]] = 1
    bz, by = bump(depth), bump(side)
    win = np.zeros((17, 24, LANES), np.float32)
    win_out = np.zeros((16, 1, depth * fine), np.float32)
    for i in range(4):
        for j in range(4):
            rows = by[2 * hb * i : 2 * hb * (i + 1)]
            cols = by[2 * hb * j : 2 * hb * (j + 1)]
            win_out[i * 4 + j, 0] = (bz[:, None, None] * rows[None, :, None] * cols[None, None, :]).reshape(-1)
            for py in range(2):
                for px in range(2):
                    value = bz[:, None] * (rows[2 * yc + py] * cols[2 * xc + px])[None]
                    win[i * 4 + j, 8 * py + px * 4 : 8 * py + px * 4 + 4] = value[:, :LANES]
                    for k in range(3):
                        at = rest * (3 * py + k)
                        win[i * 4 + j, 16 + px * 4 : 20 + px * 4, at : at + rest] = value[:, LANES:]
    return (
        jnp.asarray(place, BF16),
        jnp.asarray(spread, BF16),
        jnp.asarray(win, F32),
        jnp.asarray(win_out, F32),
    )


def shifted(values, offset):
    rows, length = values.shape
    zeros = jnp.zeros((rows, abs(offset)), values.dtype)
    if offset > 0:
        return jnp.concatenate([values[:, offset:], zeros], axis=1)
    return jnp.concatenate([zeros, values[:, : length + offset]], axis=1)


def dot(a, b):
    return jnp.dot(a, b, preferred_element_type=F32)


def split(values):
    high = values.astype(BF16)
    return high, (values - high.astype(F32)).astype(BF16)


def kernel(
    n, half,
    feat_h, w_in_h, w_plane_h, w_depth_h, w_head_h, owner_h, anchor_h, code_h, place_h, spread_h, win_h, win_out_h,
    out,
    feat, w_in, w_plane, w_depth, w_head, owner_s, anchor_s, code_s, arg_sem,
    place, spread, win, win_out, table_sem,
    wi_s, wp_s, wd_s, wh_s, xs, first_s, second_s, br0, br1,
    say, heard, inverse_v, inverse_s, inverse_sem, say_sem, hear_sem,
    pair_out0, pair_in0, kept0, cross_out0, cross_in0,
    pair_out1, pair_in1, kept1, cross_out1, cross_in1,
    pair_send, pair_recv, cross_send, cross_recv,
):
    hidden = w_in.shape[0]
    cin = w_in.shape[1]
    depth = feat.shape[2]
    plane = half * half
    block = plane // 4
    chips = n // 2
    brick_rows = n // 4
    rest = plane // 16 - LANES
    fine = plane // 4
    me = lax.axis_index("patch")
    chip, core = me // 2, lax.rem(me, 2)
    partner = me + 1 - 2 * core
    tiles = [slice(at, at + TILE) for at in range(0, plane, TILE)]

    quarters = [pl.ds(at, cin // 4) for at in range(0, cin, cin // 4)]
    arguments = [
        pltpu.make_async_copy(h, v, arg_sem.at[s])
        for s, (h, v) in enumerate(
            (
                (owner_h, owner_s), (anchor_h, anchor_s), (code_h, code_s), (w_in_h, w_in),
                (w_plane_h, w_plane), (w_depth_h, w_depth), (w_head_h, w_head),
                *[(feat_h.at[:, some], feat.at[:, some]) for some in quarters],
            )
        )
    ]
    for argument in arguments:
        argument.start()
    loads = [
        pltpu.make_async_copy(h, v, table_sem.at[s])
        for s, (h, v) in enumerate(
            (
                *[(place_h.at[flip], place.at[flip]) for flip in range(4)],
                (win_h, win), (spread_h.at[0], spread.at[0]), (spread_h.at[1], spread.at[1]), (win_out_h, win_out),
            )
        )
    ]
    barrier = pltpu.get_barrier_semaphore()
    for off in range(1, n):
        pl.semaphore_signal(barrier, inc=1, device_id={"patch": lax.rem(me + off, n)}, device_id_type=MESH)

    for argument in arguments:
        argument.wait()
    for load in loads:
        load.start()
    code = code_s[0]
    anchor = anchor_s[0]
    fz, fy, fx = code % 2, (code // 2) % 2, code // 4
    word = jnp.concatenate(
        [jnp.full((1, LANES), owner_s[0], jnp.int32), jnp.full((1, LANES), anchor, jnp.int32)], axis=0
    )
    say[...] = word
    heard[me] = word

    spread_cols = lax.broadcasted_iota(jnp.int32, (cin, cin * depth), 1) // depth
    spread_rows = lax.broadcasted_iota(jnp.int32, (cin, cin * depth), 0)
    wi_all = dot(w_in[...], (spread_cols == spread_rows).astype(F32).astype(BF16))
    section = lax.broadcasted_iota(jnp.int32, (hidden, cin * depth), 1) % depth
    wi_s[...] = jnp.zeros_like(wi_s)
    for z in range(depth):
        wi_s[PAD * z : PAD * z + hidden, :] = jnp.where(section == z, wi_all, 0.0)
    project = wi_s[...].astype(BF16)
    parts = []
    for cols in tiles:
        parts.append(dot(project, feat[0, :, :, cols].reshape(cin * depth, TILE)).astype(BF16))
    x = jnp.concatenate(parts, axis=1)
    lane_x = lax.broadcasted_iota(jnp.int32, (1, plane), 1) % half
    left = shifted(x, -1) * (lane_x >= 1).astype(F32).astype(BF16)
    right = shifted(x, 1) * (lane_x <= half - 2).astype(F32).astype(BF16)
    for dx, values in enumerate((left, x, right)):
        xs[0, dx] = shifted(values, -half)
        xs[1, dx] = values
        xs[2, dx] = shifted(values, half)

    wp_s[...] = jnp.zeros_like(wp_s)
    taps = [w_plane[t].astype(F32) for t in range(9)]
    halves = (((0,), (1, 2)), ((0, 1), (2,)))
    for sy in range(2):
        for dyi in range(2):
            for px in range(2):
                for at, txs in enumerate(halves[px]):
                    total = sum(taps[3 * ty + tx] for ty in halves[sy][dyi] for tx in txs)
                    col = PAD * (3 * dyi + px + at)
                    wp_s[sy, PAD * px : PAD * px + hidden, col : col + hidden] = total
    wd_s[...] = jnp.zeros_like(wd_s)
    for z in range(2 * depth):
        for tz in range(3):
            if (z + tz - 1) // depth == z // depth:
                col = PAD * (z + tz - 1)
                wd_s[PAD * z : PAD * z + hidden, col : col + hidden] = w_depth[tz].astype(F32)
    wh_s[...] = jnp.zeros_like(wh_s)
    for m in range(2 * depth):
        wh_s[:, PAD * m : PAD * m + hidden] = w_head[...].astype(F32)
    row8 = lax.broadcasted_iota(jnp.int32, (8, 2 * depth * PAD), 0)
    col8 = lax.broadcasted_iota(jnp.int32, (8, 2 * depth * PAD), 1) // PAD
    z_from = jnp.where(fz == 1, depth - 1 - col8 % depth, col8 % depth)
    px_from = jnp.where(fx == 1, 1 - col8 // depth, col8 // depth)
    wanted = row8 == px_from * depth + z_from
    head = jnp.concatenate(
        [jnp.where(wanted, jnp.broadcast_to(wh_s[k : k + 1, :], wanted.shape), 0.0) for k in range(3)], axis=0
    ).astype(BF16)
    depth_w = wd_s[...].astype(BF16)

    pl.semaphore_wait(barrier, n - 1)
    tells = []
    for off in range(1, n):
        tells.append(
            pltpu.make_async_remote_copy(
                src_ref=say, dst_ref=heard.at[me], send_sem=say_sem.at[off - 1], recv_sem=hear_sem.at[off - 1],
                device_id={"patch": lax.rem(me + off, n)}, device_id_type=MESH,
            )
        )
        tells[-1].start()

    lane = lax.broadcasted_iota(jnp.int32, (8, LANES), 1) // rest

    def planes(qy):
        sy = jnp.where(fy == 1, 1 - qy, qy)
        w_high, w_low = split(wp_s[sy])
        weights = jnp.concatenate([w_high, w_low], axis=0)
        for cols in tiles:
            for z in range(depth):
                rows = slice(PAD * z, PAD * (z + 1))
                around = [xs[sy + dyi, dx, rows, cols] for dyi in range(2) for dx in range(3)]
                mixed = dot(weights, jnp.concatenate(around, axis=0))
                mixed = mixed[: 2 * PAD] + mixed[2 * PAD :]
                up = xs[1, 1, rows, cols].astype(F32)
                for px in range(2):
                    first = up + jnp.maximum(mixed[PAD * px : PAD * (px + 1)], 0.0)
                    at = PAD * (depth * px + z)
                    first_s[at : at + PAD, cols] = first.astype(BF16)

    def heads(qy, brick):
        for cols in tiles:
            first = first_s[:, cols]
            second = first.astype(F32) + jnp.maximum(dot(depth_w, first), 0.0)
            second_s[:, cols] = second.astype(BF16)
        both = []
        for cols in tiles:
            affinity = jax.nn.sigmoid(dot(head, second_s[:, cols]))
            both.append(jnp.concatenate(split(affinity), axis=0))
        both = jnp.concatenate(both, axis=1)
        stacked = jnp.concatenate([both[:, block * i : block * (i + 1)] for i in range(4)], axis=0)
        if qy == 0:
            for load in loads[:4]:
                load.wait()
        placed = dot(stacked, place[code // 2])
        for i in range(4):
            value = placed[48 * i : 48 * i + 24] + placed[48 * i + 24 : 48 * i + 48]
            for j in range(4):
                e = 4 * i + j
                brick[e, 0:24, :] = value[:, LANES * j : LANES * (j + 1)]
                tail = value[:, LANES * (4 + j) : LANES * (5 + j)]
                tail = sum(jnp.where(lane == 3 * qy + k, tail[8 * k : 8 * k + 8], 0.0) for k in range(3))
                if qy == 0:
                    br1[e, 24:32, :] = tail
                else:
                    br1[e, 24:32, :] = br1[e, 24:32, :] + tail

    def piece(qy, brick, v):
        window = win[inverse_s[2, v]]
        part = window[8 * qy : 8 * qy + 8]
        window = jnp.concatenate([part] * 3 + ([window[16:24]] if qy else []), axis=0)
        return brick[inverse_s[1, v]] * window

    cut = chips // 2
    spans = (slice(0, cut), slice(cut, chips))

    def pair_start(qy, brick, pair_out, pair_in, kept):
        copies = []
        for part, span in enumerate(spans):
            for slot in range(span.start, span.stop):
                pair_out[slot] = piece(qy, brick, 2 * lax.rem(chip + slot + 1, chips) + 1 - core)
            window = pl.ds(span.start, span.stop - span.start)
            copies.append(
                pltpu.make_async_remote_copy(
                    src_ref=pair_out.at[window], dst_ref=pair_in.at[window],
                    send_sem=pair_send.at[qy, part], recv_sem=pair_recv.at[qy, part],
                    device_id={"patch": partner}, device_id_type=MESH,
                )
            )
            copies[-1].start()
        for slot in range(chips):
            kept[slot] = piece(qy, brick, 2 * lax.rem(chip + slot + 1, chips) + core)
        return copies

    def cross_start(qy, pairs, pair_in, kept, cross_out, cross_in):
        copies = []
        for pair, span in zip(pairs, spans):
            pair.wait()
            for slot in range(span.start, min(span.stop, chips - 1)):
                cross_out[slot] = kept[slot] + pair_in[slot]
                copies.append(
                    pltpu.make_async_remote_copy(
                        src_ref=cross_out.at[slot], dst_ref=cross_in.at[slot],
                        send_sem=cross_send.at[qy, slot], recv_sem=cross_recv.at[qy, slot],
                        device_id={"patch": 2 * lax.rem(chip + slot + 1, chips) + core}, device_id_type=MESH,
                    )
                )
                copies[-1].start()
        return copies

    def cross_end(copies, pair_in, kept, cross_in):
        total = kept[chips - 1] + pair_in[chips - 1]
        for at, copy in enumerate(copies):
            copy.wait()
            total = total + cross_in[at]
        return total

    planes(0)
    for tell in tells:
        tell.wait()
    lane1 = lax.broadcasted_iota(jnp.int32, (1, LANES), 1)
    inverse = sum(jnp.where(heard[d, 0:1, :] == lane1, d, 0) for d in range(n))
    i = inverse // 4 - anchor
    i = jnp.where(i < 0, i + brick_rows, i)
    j = inverse % 4
    held_i = jnp.minimum(i, 3)
    inverse_v[0:1, :] = inverse
    inverse_v[1:2, :] = 4 * jnp.where(fy == 1, 3 - held_i, held_i) + j
    inverse_v[2:3, :] = jnp.where(i < 4, 4 * held_i + j, 16)
    inverse_v[3:8, :] = jnp.zeros((5, LANES), jnp.int32)
    fetch = pltpu.make_async_copy(inverse_v, inverse_s, inverse_sem)
    fetch.start()
    heads(0, br0)
    fetch.wait()
    loads[4].wait()
    pair0 = pair_start(0, br0, pair_out0, pair_in0, kept0)
    planes(1)
    cross0 = cross_start(0, pair0, pair_in0, kept0, cross_out0, cross_in0)
    heads(1, br1)
    pair1 = pair_start(1, br1, pair_out1, pair_in1, kept1)
    cross1 = cross_start(1, pair1, pair_in1, kept1, cross_out1, cross_in1)

    for load in loads[5:]:
        load.wait()
    mine = inverse_s[0, me]
    window = jnp.zeros((1, win_out.shape[2]), F32)
    for i in range(4):
        count = jnp.zeros((1, LANES), F32)
        for d in range(n):
            at = mine // 4 - heard[d, 1:2, :]
            at = jnp.where(at < 0, at + brick_rows, at)
            count = count + jnp.where(at == i, 1.0, 0.0)
        window = window + count[:, 0:1] * win_out[4 * i + lax.rem(mine, 4)]
    out[0, 3:4, :] = window

    right_px = lax.broadcasted_iota(jnp.int32, (24, LANES), 0) // 4 % 2 == 1

    def by_px(values):
        return [jnp.where(right_px, 0.0, values), jnp.where(right_px, values, 0.0)]

    def put(values, spreading):
        both = dot(jnp.concatenate(split(jnp.concatenate(values, axis=1)), axis=0), spreading)
        return both[:24] + both[24:]

    result = put(by_px(cross_end(cross0, pair_in0, kept0, cross_in0)), spread[0, 0 : 2 * LANES, :])
    total = cross_end(cross1, pair_in1, kept1, cross_in1)
    tail = total[24:32]
    tails = [
        jnp.concatenate([jnp.where(lane == 3 * py + k, tail, 0.0) for k in range(3)], axis=0) for py in range(2)
    ]
    result = result + put(by_px(tails[0]), spread[0, 2 * LANES :, :])
    result = result + put(by_px(total[0:24]) + by_px(tails[1]), spread[1])
    for k in range(3):
        for z in range(depth):
            row = 8 * k + z
            out[0, k : k + 1, fine * z : fine * (z + 1)] = result[row : row + 1] + result[row + 4 : row + 5]


def on_device(features, w_in, w_plane, w_depth, w_head, brick_owner, patch_anchor, aug_code):
    n = lax.axis_size("patch")
    _, cin, depth, plane = features.shape
    half = math.isqrt(plane)
    block = plane // 4
    chips = n // 2
    place, spread, win, win_out = tables(half, depth)
    vmem = pl.BlockSpec(memory_space=pltpu.VMEM)
    hbm = pl.BlockSpec(memory_space=pltpu.HBM)
    rows = depth * PAD
    V = pltpu.VMEM
    dma = pltpu.SemaphoreType.DMA
    exchange = []
    for height in (24, 32):
        exchange += [V((chips, height, LANES), F32)] * 3 + [V((chips - 1, height, LANES), F32)] * 2
    return pl.pallas_call(
        functools.partial(kernel, n, half),
        out_shape=jax.ShapeDtypeStruct((1, 4, plane), F32),
        in_specs=[hbm] * 12,
        out_specs=vmem,
        scratch_shapes=[
            V(features.shape, BF16), V(w_in.shape, BF16), V(w_plane.shape, BF16), V(w_depth.shape, BF16),
            V(w_head.shape, BF16), *[pltpu.SMEM((1,), jnp.int32)] * 3, dma((11,)),
            V(place.shape, BF16), V(spread.shape, BF16), V(win.shape, F32), V(win_out.shape, F32), dma((8,)),
            V((rows, cin * depth), F32), V((2, 2 * PAD, 6 * PAD), F32), V((2 * rows, 2 * rows), F32), V((3, 2 * rows), F32),
            V((3, 3, rows, plane), BF16), V((2 * rows, plane), BF16), V((2 * rows, plane), BF16),
            V((16, 24, LANES), F32), V((16, 32, LANES), F32),
            V((2, LANES), jnp.int32), V((n, 2, LANES), jnp.int32), V((8, LANES), jnp.int32),
            pltpu.SMEM((8, LANES), jnp.int32), dma, dma((n - 1,)), dma((n - 1,)),
            *exchange,
            dma((2, 2)), dma((2, 2)), dma((2, chips - 1)), dma((2, chips - 1)),
        ],
        compiler_params=pltpu.CompilerParams(
            collective_id=0, has_side_effects=True, vmem_limit_bytes=60 * 1024 * 1024
        ),
        cost_estimate=pl.CostEstimate(flops=6_000_000_000, bytes_accessed=8_000_000, transcendentals=110_592),
    )(features, w_in, w_plane, w_depth, w_head, brick_owner, patch_anchor, aug_code, place, spread, win, win_out)


def solution(mesh):
    in_specs = (
        P(("group", "patch"), None, None, None),
        P(),
        P(),
        P(),
        P(),
        P(("group", "patch")),
        P(("group", "patch")),
        P(("group", "patch")),
    )
    out_specs = P(("group", "patch"), None, None)
    return jax.shard_map(
        on_device, mesh=mesh, in_specs=in_specs, out_specs=out_specs, check_vma=False
    )
```

```python
import functools
import math

import jax
import jax.numpy as jnp
import numpy as np
from jax import lax
from jax.experimental import pallas as pl
from jax.experimental.pallas import tpu as pltpu
from jax.sharding import PartitionSpec as P

MESH = pl.DeviceIdType.MESH
LANES = 128
TILE = 768
PAD = 32
F32 = jnp.float32
BF16 = jnp.bfloat16


def bump(length):
    position = (np.arange(length) + 0.5) / length
    return 0.1 + np.sin(np.pi * position) ** 2


def tables(half, depth):
    hb = half // 4
    cells = hb * hb
    rest = cells - LANES
    block = hb * half
    side = 2 * half
    fine = 4 * cells
    yc, xc = np.divmod(np.arange(cells), hb)
    groups = LANES // rest
    place = np.zeros((4, block, 8 * LANES), np.float32)
    for flip in range(4):
        fy, fx = flip % 2, flip // 2
        for j in range(4):
            ys = hb - 1 - yc if fy else yc
            xs = half - 1 - (hb * j + xc) if fx else hb * j + xc
            lane = ys * half + xs
            m = np.arange(LANES)
            place[flip, lane[:LANES], j * LANES + m] = 1
            for g in range(groups):
                place[flip, lane[LANES:], (4 + j) * LANES + rest * g + np.arange(rest)] = 1
    spread = np.zeros((2, 4 * LANES, fine), np.float32)
    for py in range(2):
        for px in range(2):
            cell = (2 * yc + py) * (2 * hb) + 2 * xc + px
            spread[py, px * LANES + np.arange(LANES), cell[:LANES]] = 1
            for g in range(groups):
                spread[py, (2 + px) * LANES + rest * g + np.arange(rest), cell[LANES:]] = 1
    bz, by = bump(depth), bump(side)
    win = np.zeros((17, 24, LANES), np.float32)
    win_out = np.zeros((16, 1, depth * fine), np.float32)
    for i in range(4):
        for j in range(4):
            rows = by[2 * hb * i : 2 * hb * (i + 1)]
            cols = by[2 * hb * j : 2 * hb * (j + 1)]
            win_out[i * 4 + j, 0] = (bz[:, None, None] * rows[None, :, None] * cols[None, None, :]).reshape(-1)
            for py in range(2):
                for px in range(2):
                    value = bz[:, None] * (rows[2 * yc + py] * cols[2 * xc + px])[None]
                    win[i * 4 + j, 8 * py + px * 4 : 8 * py + px * 4 + 4] = value[:, :LANES]
                    for k in range(3):
                        at = rest * (3 * py + k)
                        win[i * 4 + j, 16 + px * 4 : 20 + px * 4, at : at + rest] = value[:, LANES:]
    return (
        jnp.asarray(place, BF16),
        jnp.asarray(spread, BF16),
        jnp.asarray(win, F32),
        jnp.asarray(win_out, F32),
    )


def shifted(values, offset):
    rows, length = values.shape
    zeros = jnp.zeros((rows, abs(offset)), values.dtype)
    if offset > 0:
        return jnp.concatenate([values[:, offset:], zeros], axis=1)
    return jnp.concatenate([zeros, values[:, : length + offset]], axis=1)


def dot(a, b):
    return jnp.dot(a, b, preferred_element_type=F32)


def split(values):
    high = values.astype(BF16)
    return high, (values - high.astype(F32)).astype(BF16)


def kernel(
    n, half,
    feat_h, w_in_h, w_plane_h, w_depth_h, w_head_h, owner_h, anchor_h, code_h, place_h, spread_h, win_h, win_out_h,
    out,
    feat, w_in, w_plane, w_depth, w_head, owner_s, anchor_s, code_s, arg_sem,
    place, spread, win, win_out, table_sem,
    wi_s, wp_s, wd_s, wh_s, xs, first_s, second_s, br0, br1,
    say, heard, inverse_v, inverse_s, inverse_sem, say_sem, hear_sem,
    pair_out0, pair_in0, kept0, cross_out0, cross_in0,
    pair_out1, pair_in1, kept1, cross_out1, cross_in1,
    pair_send, pair_recv, cross_send, cross_recv,
):
    hidden = w_in.shape[0]
    cin = w_in.shape[1]
    depth = feat.shape[2]
    plane = half * half
    block = plane // 4
    chips = n // 2
    brick_rows = n // 4
    rest = plane // 16 - LANES
    fine = plane // 4
    me = lax.axis_index("patch")
    chip, core = me // 2, lax.rem(me, 2)
    partner = me + 1 - 2 * core
    tiles = [slice(at, at + TILE) for at in range(0, plane, TILE)]

    quarters = [pl.ds(at, cin // 4) for at in range(0, cin, cin // 4)]
    arguments = [
        pltpu.make_async_copy(h, v, arg_sem.at[s])
        for s, (h, v) in enumerate(
            (
                (owner_h, owner_s), (anchor_h, anchor_s), (code_h, code_s), (w_in_h, w_in),
                (w_plane_h, w_plane), (w_depth_h, w_depth), (w_head_h, w_head),
                *[(feat_h.at[:, some], feat.at[:, some]) for some in quarters],
            )
        )
    ]
    for argument in arguments:
        argument.start()
    loads = [
        pltpu.make_async_copy(h, v, table_sem.at[s])
        for s, (h, v) in enumerate(
            (
                *[(place_h.at[flip], place.at[flip]) for flip in range(4)],
                (win_h, win), (spread_h.at[0], spread.at[0]), (spread_h.at[1], spread.at[1]), (win_out_h, win_out),
            )
        )
    ]
    barrier = pltpu.get_barrier_semaphore()
    for off in range(1, n):
        pl.semaphore_signal(barrier, inc=1, device_id={"patch": lax.rem(me + off, n)}, device_id_type=MESH)

    for argument in arguments:
        argument.wait()
    for load in loads:
        load.start()
    code = code_s[0]
    anchor = anchor_s[0]
    fz, fy, fx = code % 2, (code // 2) % 2, code // 4
    word = jnp.concatenate(
        [jnp.full((1, LANES), owner_s[0], jnp.int32), jnp.full((1, LANES), anchor, jnp.int32)], axis=0
    )
    say[...] = word
    heard[me] = word

    spread_cols = lax.broadcasted_iota(jnp.int32, (cin, cin * depth), 1) // depth
    spread_rows = lax.broadcasted_iota(jnp.int32, (cin, cin * depth), 0)
    wi_all = dot(w_in[...], (spread_cols == spread_rows).astype(F32).astype(BF16))
    section = lax.broadcasted_iota(jnp.int32, (hidden, cin * depth), 1) % depth
    wi_s[...] = jnp.zeros_like(wi_s)
    for z in range(depth):
        wi_s[PAD * z : PAD * z + hidden, :] = jnp.where(section == z, wi_all, 0.0)
    project = wi_s[...].astype(BF16)
    parts = []
    for cols in tiles:
        parts.append(dot(project, feat[0, :, :, cols].reshape(cin * depth, TILE)).astype(BF16))
    x = jnp.concatenate(parts, axis=1)
    lane_x = lax.broadcasted_iota(jnp.int32, (1, plane), 1) % half
    left = shifted(x, -1) * (lane_x >= 1).astype(F32).astype(BF16)
    right = shifted(x, 1) * (lane_x <= half - 2).astype(F32).astype(BF16)
    for dx, values in enumerate((left, x, right)):
        xs[0, dx] = shifted(values, -half)
        xs[1, dx] = values
        xs[2, dx] = shifted(values, half)

    wp_s[...] = jnp.zeros_like(wp_s)
    taps = [w_plane[t].astype(F32) for t in range(9)]
    halves = (((0,), (1, 2)), ((0, 1), (2,)))
    for sy in range(2):
        for dyi in range(2):
            for px in range(2):
                for at, txs in enumerate(halves[px]):
                    total = sum(taps[3 * ty + tx] for ty in halves[sy][dyi] for tx in txs)
                    col = PAD * (3 * dyi + px + at)
                    wp_s[sy, PAD * px : PAD * px + hidden, col : col + hidden] = total
    wd_s[...] = jnp.zeros_like(wd_s)
    for z in range(2 * depth):
        for tz in range(3):
            if (z + tz - 1) // depth == z // depth:
                col = PAD * (z + tz - 1)
                wd_s[PAD * z : PAD * z + hidden, col : col + hidden] = w_depth[tz].astype(F32)
    wh_s[...] = jnp.zeros_like(wh_s)
    for m in range(2 * depth):
        wh_s[:, PAD * m : PAD * m + hidden] = w_head[...].astype(F32)
    row8 = lax.broadcasted_iota(jnp.int32, (8, 2 * depth * PAD), 0)
    col8 = lax.broadcasted_iota(jnp.int32, (8, 2 * depth * PAD), 1) // PAD
    z_from = jnp.where(fz == 1, depth - 1 - col8 % depth, col8 % depth)
    px_from = jnp.where(fx == 1, 1 - col8 // depth, col8 // depth)
    wanted = row8 == px_from * depth + z_from
    head = jnp.concatenate(
        [jnp.where(wanted, jnp.broadcast_to(wh_s[k : k + 1, :], wanted.shape), 0.0) for k in range(3)], axis=0
    ).astype(BF16)
    depth_w = wd_s[...].astype(BF16)

    pl.semaphore_wait(barrier, n - 1)
    tells = []
    for off in range(1, n):
        tells.append(
            pltpu.make_async_remote_copy(
                src_ref=say, dst_ref=heard.at[me], send_sem=say_sem.at[off - 1], recv_sem=hear_sem.at[off - 1],
                device_id={"patch": lax.rem(me + off, n)}, device_id_type=MESH,
            )
        )
        tells[-1].start()

    lane = lax.broadcasted_iota(jnp.int32, (8, LANES), 1) // rest

    def planes(qy):
        sy = jnp.where(fy == 1, 1 - qy, qy)
        w_high, w_low = split(wp_s[sy])
        weights = jnp.concatenate([w_high, w_low], axis=0)
        for cols in tiles:
            for z in range(depth):
                rows = slice(PAD * z, PAD * (z + 1))
                around = [xs[sy + dyi, dx, rows, cols] for dyi in range(2) for dx in range(3)]
                mixed = dot(weights, jnp.concatenate(around, axis=0))
                mixed = mixed[: 2 * PAD] + mixed[2 * PAD :]
                up = xs[1, 1, rows, cols].astype(F32)
                for px in range(2):
                    first = up + jnp.maximum(mixed[PAD * px : PAD * (px + 1)], 0.0)
                    at = PAD * (depth * px + z)
                    first_s[at : at + PAD, cols] = first.astype(BF16)

    def heads(qy, brick):
        for cols in tiles:
            first = first_s[:, cols]
            second = first.astype(F32) + jnp.maximum(dot(depth_w, first), 0.0)
            second_s[:, cols] = second.astype(BF16)
        both = []
        for cols in tiles:
            affinity = jax.nn.sigmoid(dot(head, second_s[:, cols]))
            both.append(jnp.concatenate(split(affinity), axis=0))
        both = jnp.concatenate(both, axis=1)
        stacked = jnp.concatenate([both[:, block * i : block * (i + 1)] for i in range(4)], axis=0)
        if qy == 0:
            for load in loads[:4]:
                load.wait()
        placed = dot(stacked, place[code // 2])
        for i in range(4):
            value = placed[48 * i : 48 * i + 24] + placed[48 * i + 24 : 48 * i + 48]
            for j in range(4):
                e = 4 * i + j
                brick[e, 0:24, :] = value[:, LANES * j : LANES * (j + 1)]
                tail = value[:, LANES * (4 + j) : LANES * (5 + j)]
                tail = sum(jnp.where(lane == 3 * qy + k, tail[8 * k : 8 * k + 8], 0.0) for k in range(3))
                if qy == 0:
                    br1[e, 24:32, :] = tail
                else:
                    br1[e, 24:32, :] = br1[e, 24:32, :] + tail

    def piece(qy, brick, v):
        window = win[inverse_s[2, v]]
        part = window[8 * qy : 8 * qy + 8]
        window = jnp.concatenate([part] * 3 + ([window[16:24]] if qy else []), axis=0)
        return brick[inverse_s[1, v]] * window

    cut = chips // 2
    spans = (slice(0, cut), slice(cut, chips))

    def pair_start(qy, brick, pair_out, pair_in, kept):
        copies = []
        for part, span in enumerate(spans):
            for slot in range(span.start, span.stop):
                pair_out[slot] = piece(qy, brick, 2 * lax.rem(chip + slot + 1, chips) + 1 - core)
            window = pl.ds(span.start, span.stop - span.start)
            copies.append(
                pltpu.make_async_remote_copy(
                    src_ref=pair_out.at[window], dst_ref=pair_in.at[window],
                    send_sem=pair_send.at[qy, part], recv_sem=pair_recv.at[qy, part],
                    device_id={"patch": partner}, device_id_type=MESH,
                )
            )
            copies[-1].start()
        for slot in range(chips):
            kept[slot] = piece(qy, brick, 2 * lax.rem(chip + slot + 1, chips) + core)
        return copies

    def cross_start(qy, pairs, pair_in, kept, cross_out, cross_in):
        copies = []
        for pair, span in zip(pairs, spans):
            pair.wait()
            for slot in range(span.start, min(span.stop, chips - 1)):
                cross_out[slot] = kept[slot] + pair_in[slot]
                copies.append(
                    pltpu.make_async_remote_copy(
                        src_ref=cross_out.at[slot], dst_ref=cross_in.at[slot],
                        send_sem=cross_send.at[qy, slot], recv_sem=cross_recv.at[qy, slot],
                        device_id={"patch": 2 * lax.rem(chip + slot + 1, chips) + core}, device_id_type=MESH,
                    )
                )
                copies[-1].start()
        return copies

    def cross_end(copies, pair_in, kept, cross_in):
        total = kept[chips - 1] + pair_in[chips - 1]
        for at, copy in enumerate(copies):
            copy.wait()
            total = total + cross_in[at]
        return total

    planes(0)
    for tell in tells:
        tell.wait()
    lane1 = lax.broadcasted_iota(jnp.int32, (1, LANES), 1)
    inverse = sum(jnp.where(heard[d, 0:1, :] == lane1, d, 0) for d in range(n))
    i = inverse // 4 - anchor
    i = jnp.where(i < 0, i + brick_rows, i)
    j = inverse % 4
    held_i = jnp.minimum(i, 3)
    inverse_v[0:1, :] = inverse
    inverse_v[1:2, :] = 4 * jnp.where(fy == 1, 3 - held_i, held_i) + j
    inverse_v[2:3, :] = jnp.where(i < 4, 4 * held_i + j, 16)
    inverse_v[3:8, :] = jnp.zeros((5, LANES), jnp.int32)
    fetch = pltpu.make_async_copy(inverse_v, inverse_s, inverse_sem)
    fetch.start()
    heads(0, br0)
    fetch.wait()
    loads[4].wait()
    pair0 = pair_start(0, br0, pair_out0, pair_in0, kept0)
    planes(1)
    cross0 = cross_start(0, pair0, pair_in0, kept0, cross_out0, cross_in0)
    heads(1, br1)
    pair1 = pair_start(1, br1, pair_out1, pair_in1, kept1)
    cross1 = cross_start(1, pair1, pair_in1, kept1, cross_out1, cross_in1)

    for load in loads[5:]:
        load.wait()
    mine = inverse_s[0, me]
    window = jnp.zeros((1, win_out.shape[2]), F32)
    for i in range(4):
        count = jnp.zeros((1, LANES), F32)
        for d in range(n):
            at = mine // 4 - heard[d, 1:2, :]
            at = jnp.where(at < 0, at + brick_rows, at)
            count = count + jnp.where(at == i, 1.0, 0.0)
        window = window + count[:, 0:1] * win_out[4 * i + lax.rem(mine, 4)]
    out[0, 3:4, :] = window

    right_px = lax.broadcasted_iota(jnp.int32, (24, LANES), 0) // 4 % 2 == 1

    def by_px(values):
        return [jnp.where(right_px, 0.0, values), jnp.where(right_px, values, 0.0)]

    def put(values, spreading):
        both = dot(jnp.concatenate(split(jnp.concatenate(values, axis=1)), axis=0), spreading)
        return both[:24] + both[24:]

    result = put(by_px(cross_end(cross0, pair_in0, kept0, cross_in0)), spread[0, 0 : 2 * LANES, :])
    total = cross_end(cross1, pair_in1, kept1, cross_in1)
    tail = total[24:32]
    tails = [
        jnp.concatenate([jnp.where(lane == 3 * py + k, tail, 0.0) for k in range(3)], axis=0) for py in range(2)
    ]
    result = result + put(by_px(tails[0]), spread[0, 2 * LANES :, :])
    result = result + put(by_px(total[0:24]) + by_px(tails[1]), spread[1])
    for k in range(3):
        for z in range(depth):
            row = 8 * k + z
            out[0, k : k + 1, fine * z : fine * (z + 1)] = result[row : row + 1] + result[row + 4 : row + 5]


def on_device(features, w_in, w_plane, w_depth, w_head, brick_owner, patch_anchor, aug_code):
    n = lax.axis_size("patch")
    _, cin, depth, plane = features.shape
    half = math.isqrt(plane)
    block = plane // 4
    chips = n // 2
    place, spread, win, win_out = tables(half, depth)
    vmem = pl.BlockSpec(memory_space=pltpu.VMEM)
    hbm = pl.BlockSpec(memory_space=pltpu.HBM)
    rows = depth * PAD
    V = pltpu.VMEM
    dma = pltpu.SemaphoreType.DMA
    exchange = []
    for height in (24, 32):
        exchange += [V((chips, height, LANES), F32)] * 3 + [V((chips - 1, height, LANES), F32)] * 2
    return pl.pallas_call(
        functools.partial(kernel, n, half),
        out_shape=jax.ShapeDtypeStruct((1, 4, plane), F32),
        in_specs=[hbm] * 12,
        out_specs=vmem,
        scratch_shapes=[
            V(features.shape, BF16), V(w_in.shape, BF16), V(w_plane.shape, BF16), V(w_depth.shape, BF16),
            V(w_head.shape, BF16), *[pltpu.SMEM((1,), jnp.int32)] * 3, dma((11,)),
            V(place.shape, BF16), V(spread.shape, BF16), V(win.shape, F32), V(win_out.shape, F32), dma((8,)),
            V((rows, cin * depth), F32), V((2, 2 * PAD, 6 * PAD), F32), V((2 * rows, 2 * rows), F32), V((3, 2 * rows), F32),
            V((3, 3, rows, plane), BF16), V((2 * rows, plane), BF16), V((2 * rows, plane), BF16),
            V((16, 24, LANES), F32), V((16, 32, LANES), F32),
            V((2, LANES), jnp.int32), V((n, 2, LANES), jnp.int32), V((8, LANES), jnp.int32),
            pltpu.SMEM((8, LANES), jnp.int32), dma, dma((n - 1,)), dma((n - 1,)),
            *exchange,
            dma((2, 2)), dma((2, 2)), dma((2, chips - 1)), dma((2, chips - 1)),
        ],
        compiler_params=pltpu.CompilerParams(
            collective_id=0, has_side_effects=True, vmem_limit_bytes=60 * 1024 * 1024
        ),
        cost_estimate=pl.CostEstimate(flops=6_000_000_000, bytes_accessed=8_000_000, transcendentals=110_592),
    )(features, w_in, w_plane, w_depth, w_head, brick_owner, patch_anchor, aug_code, place, spread, win, win_out)


def solution(mesh):
    in_specs = (
        P(("group", "patch"), None, None, None),
        P(),
        P(),
        P(),
        P(),
        P(("group", "patch")),
        P(("group", "patch")),
        P(("group", "patch")),
    )
    out_specs = P(("group", "patch"), None, None)
    return jax.shard_map(
        on_device, mesh=mesh, in_specs=in_specs, out_specs=out_specs, check_vma=False
    )
```
